32 devices in a mesh: req: 8 (over z, y), grp: 4 (over x, core).
Axes of the slice: x: 2, y: 2, z: 4, core: 2. Of those that a mesh axis runs over, the one named last changes fastest.
Arguments:
- hidden_in: bfloat16 [4096, 2048], P('req'), may hold values from -6 to 6
- attn_gain: float32 [2048], replicated, may hold values from 0.1 to 1.9
- mlp_gain: float32 [2048], replicated, may hold values from 0.1 to 1.9
- w_query: bfloat16 [2048, 2048], P(None, 'grp'), may hold values from -0.75 to 0.75
- w_key: bfloat16 [2048, 512], P(None, 'grp'), may hold values from -0.125 to 0.125
- w_value: bfloat16 [2048, 512], P(None, 'grp'), may hold values from -0.125 to 0.125
- w_out: bfloat16 [2048, 2048], P('grp'), may hold values from -0.125 to 0.125
- w_gate: bfloat16 [2048, 8192], P(None, 'req'), may hold values from -0.125 to 0.125
- w_up: bfloat16 [2048, 8192], P(None, 'req'), may hold values from -0.125 to 0.125
- w_down: bfloat16 [8192, 2048], P('req'), may hold values from -0.0625 to 0.0625
- cache_k: bfloat16 [1024, 16, 512], P('req', None, 'grp'), may hold values from -4000 to 4000
- cache_v: bfloat16 [1024, 16, 512], P('req', None, 'grp'), may hold values from -6 to 6
- owner_of_row: int32 [4096], P('req'), may hold values from 0 to 7, as said below
- new_len: int32 [8, 8], P('req'), may hold values from 0 to 128, as said below
- prior_len: int32 [8, 8], P('req'), may hold values from 0 to 256, as said below
- page_table: int32 [8, 128], P('req'), may hold values from 0 to 127, each once within a row
Outputs:
- layer_out: bfloat16 [4096, 2048], P(('req', 'grp'))
- new_cache_k: bfloat16 [1024, 16, 512], P('req', None, 'grp')
- new_cache_v: bfloat16 [1024, 16, 512], P('req', None, 'grp')
The draws below stay inside these ranges and needn't reach their ends.
Inputs may be any that keep to these rules, and one draw needn't show every extreme that they name: `owner_of_row`: rows of one block of 512 that name the same owner are consecutive; each block holds at most one request for each owner, of at most 128 rows; in every draw one owner receives a request of exactly 128 rows from every block. new_len[o, s] is the number of rows of block s of owner_of_row that name o. prior_len[o, s] + new_len[o, s] <= 256.
All inputs are finite; a program needn't handle non-finite values.
Results may differ from the reference program's by a relative error of at most 0.0063.
Values may be sent and summed in bfloat16 or wider, within the bound.
No kernel may reach another device: no remote copies, remote signals or barrier semaphores. Data moves between devices by JAX's collectives and lax.ppermute only.
A program may use at most 128 MiB of HBM per device.

```python
import jax
import jax.numpy as jnp
from jax import lax

D = 2048
HEADS = 32
KVH = 8
HD = 64
FF = 8192
ROWS = 512
PAGE = 16
MAXP = 16
TOKENS = 4096
PAIR = 128
CONTEXT = 256
POOL = 128
HEAD_BLOCKS = 4
QCOLS = 512
UNIT_BLOCKS = 8
FF_DEV = 1024
N_REQ = 8


def make_plan(key):
    hot_key = jax.random.fold_in(key, 11)
    hottest = jax.random.randint(hot_key, (), 0, N_REQ)
    owners = jnp.arange(N_REQ, dtype=jnp.int32)

    def per_source(source):
        source_key = jax.random.fold_in(key, 1000 + source)
        key_shift, key_rank, key_first, key_pack = jax.random.split(source_key, 4)
        shift = jax.random.randint(key_shift, (), 1, N_REQ)
        vacant = (hottest + shift) % N_REQ
        ranks = jax.random.permutation(key_rank, N_REQ).astype(jnp.int32)
        special = jnp.logical_or(owners == hottest, owners == vacant)
        scores = ranks + N_REQ * special.astype(jnp.int32)
        order = jnp.argsort(scores, stable=True)
        firsts = jax.random.randint(key_first, (N_REQ // 2,), 1, PAIR)
        paired = jnp.stack([firsts, PAIR - firsts], axis=1).reshape(-1)
        sorted_len = jnp.where(jnp.arange(N_REQ, dtype=jnp.int32) < N_REQ - 2, paired, 0)
        lengths = jnp.zeros((N_REQ,), jnp.int32).at[order].set(sorted_len.astype(jnp.int32))
        lengths = jnp.where(owners == hottest, PAIR, lengths)
        lengths = jnp.where(owners == vacant, 0, lengths)
        packing = jax.random.permutation(key_pack, N_REQ).astype(jnp.int32)
        ends = jnp.cumsum(lengths[packing])
        row_ids = jnp.arange(ROWS, dtype=jnp.int32)
        which = jnp.sum((ends[None, :] <= row_ids[:, None]).astype(jnp.int32), axis=1)
        return (packing[which], lengths)
    row_owner, lengths = jax.vmap(per_source)(jnp.arange(N_REQ, dtype=jnp.int32))
    return (row_owner.reshape(-1).astype(jnp.int32), jnp.transpose(lengths).astype(jnp.int32), hottest)


def draw_owner_of_row(key, part):
    return make_plan(key)[0]


def draw_new_len(key, part):
    return make_plan(key)[1]


def draw_prior_len(key, part):
    plan = make_plan(key)
    lengths = plan[1]
    hottest = plan[2]
    prior_key = jax.random.fold_in(key, 23)
    room = CONTEXT - lengths
    prior = jax.random.randint(prior_key, (N_REQ, N_REQ), 0, room + 1)
    prior = jnp.where(lengths == 0, CONTEXT, prior)
    prior = prior.at[hottest, hottest].set(0)
    return prior.astype(jnp.int32)


def draw_cache_k(key, part):
    shape = (N_REQ * POOL, PAGE, KVH * HD)
    base_key = jax.random.fold_in(key, 0)
    values = jnp.clip(jax.random.normal(base_key, shape, jnp.float32), -6.0, 6.0)
    return values.astype(jnp.bfloat16)


def block_scale(key, extent, shards, low, high):
    factor_of, own = 1.0, jax.random.fold_in(key, 6)
    for axis_at, parts in shards:
        draws = jnp.exp(jax.random.uniform(jax.random.fold_in(own, axis_at), (parts,), jnp.float32, low / len(shards), high / len(shards)))
        factor_of = factor_of * jnp.repeat(draws, extent[axis_at] // parts).reshape([-1 if axis == axis_at else 1 for axis in range(len(extent))])
    return factor_of


def normal_values(own_key, shape, scale, most, shards=(), kind=jnp.bfloat16):
    entries = scale * jax.random.normal(own_key, shape, jnp.float32)
    if shards:
        entries = entries * block_scale(own_key, shape, shards, -0.22, 0.18)
    return jnp.clip(entries, -most, most).astype(kind)


def setup_inputs(seed: int = 0) -> dict:
    key_of = jax.random.split(jax.random.key(seed), 17)
    hidden_in = normal_values(key_of[0], (TOKENS, D), 1.0, 6.0, ((0, 8),))
    attn_gain = jnp.clip(1.0 + 0.18 * jax.random.normal(key_of[1], (D,), jnp.float32), 0.1, 1.9)
    mlp_gain = jnp.clip(1.0 + 0.18 * jax.random.normal(key_of[2], (D,), jnp.float32), 0.1, 1.9)
    w_query = normal_values(key_of[3], (D, HEADS * HD), (D // 32) ** -0.5, 0.75, ((1, 4),))
    w_key = normal_values(key_of[4], (D, KVH * HD), D ** -0.5, 0.125, ((1, 4),))
    w_value = normal_values(key_of[5], (D, KVH * HD), D ** -0.5, 0.125, ((1, 4),))
    w_out = normal_values(key_of[6], (HEADS * HD, D), (HEADS * HD) ** -0.5, 0.125, ((0, 4),))
    w_gate = normal_values(key_of[7], (D, FF), D ** -0.5, 0.125, ((1, 8),))
    w_up = normal_values(key_of[8], (D, FF), D ** -0.5, 0.125, ((1, 8),))
    w_down = normal_values(key_of[9], (FF, D), FF ** -0.5, 0.0625, ((0, 8),))
    cache_k = draw_cache_k(jax.random.fold_in(key_of[16], 71), 0)
    cache_v = normal_values(key_of[11], (N_REQ * POOL, PAGE, KVH * HD), 1.0, 6.0, ((0, 8), (2, 4)))
    owner_of_row = draw_owner_of_row(jax.random.fold_in(key_of[16], 71), 0)
    new_len = draw_new_len(jax.random.fold_in(key_of[16], 71), 0)
    prior_len = draw_prior_len(jax.random.fold_in(key_of[16], 71), 0)
    page_table = jax.vmap(lambda own: jax.random.permutation(own, POOL))(jax.random.split(key_of[15], N_REQ)).reshape((N_REQ, POOL)).astype(jnp.int32)
    return {"hidden_in": hidden_in, "attn_gain": attn_gain, "mlp_gain": mlp_gain, "w_query": w_query, "w_key": w_key, "w_value": w_value, "w_out": w_out, "w_gate": w_gate, "w_up": w_up, "w_down": w_down, "cache_k": cache_k, "cache_v": cache_v, "owner_of_row": owner_of_row, "new_len": new_len, "prior_len": prior_len, "page_table": page_table}


EPSILON = 1e-05
RESIDUAL_MULT = 0.22
SCORE_MULT = 0.015625
ROPE_BASE = 10000000.0

def normalize(values, gain):
    mean_square = lax.optimization_barrier(jnp.mean(values * values, axis=-1, keepdims=True))
    return values * lax.rsqrt(mean_square + EPSILON) * gain

def rotary(values, positions):
    dim = values.shape[-1]
    half = dim // 2
    freq = jnp.power(ROPE_BASE, -2.0 * jnp.arange(half, dtype=jnp.int32).astype(jnp.float32) / dim)
    angle = positions.astype(jnp.float32)[:, :, None] * freq
    cosine = jnp.cos(angle)[:, :, None, :]
    sine = jnp.sin(angle)[:, :, None, :]
    first = values[..., :half].astype(jnp.float32)
    second = values[..., half:].astype(jnp.float32)
    return jnp.concatenate([first * cosine - second * sine, second * cosine + first * sine], axis=-1)

def source_layout(owner_block, peers, pair_rows):
    row_count = owner_block.shape[0]
    owners = jnp.arange(peers, dtype=jnp.int32)
    member = owner_block[None, :] == owners[:, None]
    counts = lax.optimization_barrier(jnp.sum(member.astype(jnp.int32), axis=1))
    row_ids = jnp.arange(row_count, dtype=jnp.int32)
    starts = lax.optimization_barrier(jnp.min(jnp.where(member, row_ids[None, :], row_count), axis=1))
    slots = jnp.arange(pair_rows, dtype=jnp.int32)
    gather_rows = jnp.where(slots[None, :] < counts[:, None], starts[:, None] + slots[None, :], row_count)
    row_start = lax.optimization_barrier(jnp.sum(jnp.where(member, starts[:, None], 0), axis=0))
    back_rows = owner_block * pair_rows + (row_ids - row_start)
    return (gather_rows.reshape(-1).astype(jnp.int32), back_rows.astype(jnp.int32))

def owner_attention(query_in, key_in, value_in, cache_keys, cache_values, lengths, priors, table):
    sources, pair_rows, qcols = query_in.shape
    kcols = key_in.shape[-1]
    kv_heads = kcols // HD
    group = qcols // kcols
    pool_pages = cache_keys.shape[0]
    slots = jnp.arange(pair_rows, dtype=jnp.int32)
    positions = priors[:, None] + slots[None, :]
    live = slots[None, :] < lengths[:, None]
    query_rot = rotary(query_in.reshape(sources, pair_rows, qcols // HD, HD), positions).astype(jnp.bfloat16)
    key_rot = rotary(key_in.reshape(sources, pair_rows, kv_heads, HD), positions).astype(jnp.bfloat16)
    key_rot = key_rot.reshape(sources, pair_rows, kcols)
    pages = table.reshape(sources, MAXP)
    page_index = jnp.minimum(positions // PAGE, MAXP - 1)
    target = jnp.take_along_axis(pages, page_index, axis=1)
    target = jnp.where(live, target, pool_pages).reshape(-1)
    offset = (positions % PAGE).reshape(-1)
    keys_out = cache_keys.at[target, offset].set(key_rot.reshape(-1, kcols), mode='drop')
    values_out = cache_values.at[target, offset].set(value_in.reshape(-1, kcols), mode='drop')
    key_block = jnp.take(keys_out, pages.reshape(-1), axis=0).reshape(sources, CONTEXT, kv_heads, HD)
    value_block = jnp.take(values_out, pages.reshape(-1), axis=0).reshape(sources, CONTEXT, kv_heads, HD)
    grouped = query_rot.reshape(sources, pair_rows, kv_heads, group, HD)
    scores = jnp.einsum('stkgd,sjkd->skgtj', grouped.astype(jnp.float32), key_block.astype(jnp.float32)) * SCORE_MULT
    allowed = jnp.arange(CONTEXT, dtype=jnp.int32)[None, None, None, None, :] <= positions[:, None, None, :, None]
    scores = jnp.where(allowed, scores, -jnp.inf)
    top = lax.optimization_barrier(jnp.max(scores, axis=-1, keepdims=True))
    weights = jnp.exp(scores - top)
    probs = (weights / lax.optimization_barrier(jnp.sum(weights, axis=-1, keepdims=True))).astype(jnp.bfloat16)
    mixed = jnp.einsum('skgtj,sjkd->stkgd', probs.astype(jnp.float32), value_block.astype(jnp.float32))
    return (mixed.astype(jnp.bfloat16).reshape(sources, pair_rows, qcols), keys_out, values_out)

def reference(hidden_in, attn_gain, mlp_gain, w_query, w_key, w_value, w_out, w_gate, w_up, w_down, cache_k, cache_v, owner_of_row, new_len, prior_len, page_table):
    inputs = hidden_in.astype(jnp.float32)
    normed = normalize(inputs, attn_gain).astype(jnp.bfloat16)
    query_all = jnp.dot(normed, w_query, preferred_element_type=jnp.float32).astype(jnp.bfloat16)
    key_all = jnp.dot(normed, w_key, preferred_element_type=jnp.float32).astype(jnp.bfloat16)
    value_all = jnp.dot(normed, w_value, preferred_element_type=jnp.float32).astype(jnp.bfloat16)
    owner_blocks = owner_of_row.reshape(N_REQ, ROWS)
    gather_rows, back_rows = jax.vmap(lambda block: source_layout(block, N_REQ, PAIR))(owner_blocks)

    def sendout(table_rows, indices):
        picked = jnp.take(table_rows, indices, axis=0, mode='fill', fill_value=0)
        return picked.reshape(N_REQ, PAIR, -1)
    send_query = jax.vmap(sendout)(query_all.reshape(N_REQ, ROWS, -1), gather_rows)
    send_key = jax.vmap(sendout)(key_all.reshape(N_REQ, ROWS, -1), gather_rows)
    send_value = jax.vmap(sendout)(value_all.reshape(N_REQ, ROWS, -1), gather_rows)
    recv_query = jnp.swapaxes(send_query, 0, 1)
    recv_key = jnp.swapaxes(send_key, 0, 1)
    recv_value = jnp.swapaxes(send_value, 0, 1)
    owner_keys = cache_k.reshape(N_REQ, POOL, PAGE, KVH * HD)
    owner_values = cache_v.reshape(N_REQ, POOL, PAGE, KVH * HD)

    def per_owner(items):
        return owner_attention(*items)
    mixed, keys_new, values_new = lax.map(per_owner, (recv_query, recv_key, recv_value, owner_keys, owner_values, new_len, prior_len, page_table))
    back = jnp.swapaxes(mixed, 0, 1).reshape(N_REQ, N_REQ * PAIR, -1)
    attn = jax.vmap(lambda block, indices: jnp.take(block, indices, axis=0))(back, back_rows).reshape(TOKENS, -1)
    attn_sum = jnp.zeros((TOKENS, D), jnp.float32)
    for block in range(HEAD_BLOCKS):
        part = jnp.dot(attn[:, block * QCOLS:(block + 1) * QCOLS], w_out[block * QCOLS:(block + 1) * QCOLS], preferred_element_type=jnp.float32)
        part = lax.optimization_barrier(part.astype(jnp.bfloat16))
        attn_sum = attn_sum + part.astype(jnp.float32)
    residual = inputs + RESIDUAL_MULT * attn_sum
    mlp_in = normalize(residual, mlp_gain).astype(jnp.bfloat16)
    gate_blocks = jnp.transpose(w_gate.reshape(D, UNIT_BLOCKS, FF_DEV), (1, 0, 2))
    up_blocks = jnp.transpose(w_up.reshape(D, UNIT_BLOCKS, FF_DEV), (1, 0, 2))
    down_blocks = w_down.reshape(UNIT_BLOCKS, FF_DEV, D)

    def add_block(total, weights):
        gate = jnp.dot(mlp_in, weights[0], preferred_element_type=jnp.float32)
        upper = jnp.dot(mlp_in, weights[1], preferred_element_type=jnp.float32)
        hidden = (jax.nn.silu(gate) * upper).astype(jnp.bfloat16)
        term = jnp.dot(hidden, weights[2], preferred_element_type=jnp.float32).astype(jnp.bfloat16)
        term = lax.optimization_barrier(term)
        return (total + term.astype(jnp.float32), None)
    down, _ = lax.scan(add_block, jnp.zeros((TOKENS, D), jnp.float32), (gate_blocks, up_blocks, down_blocks))
    layer_out = (residual + RESIDUAL_MULT * down).astype(jnp.bfloat16)
    return (layer_out, keys_new.reshape(N_REQ * POOL, PAGE, KVH * HD), values_new.reshape(N_REQ * POOL, PAGE, KVH * HD))
```

```python
import functools

import jax
import jax.numpy as jnp
from jax import lax
from jax.experimental import pallas as pl
from jax.experimental.pallas import tpu as pltpu
from jax.sharding import PartitionSpec as P

HD = 64
PAGE = 16
MAXP = 16
CONTEXT = 256
LANES = 128
INFO = 16


EPSILON = 1e-05
RESIDUAL_MULT = 0.22
SCORE_MULT = 0.015625
ROPE_BASE = 10000000.0
BF = jnp.bfloat16
F32 = jnp.float32
SMEM = pl.BlockSpec(memory_space=pltpu.SMEM)
VMEM = pl.BlockSpec(memory_space=pltpu.VMEM)


def normalize(values, gain):
    mean_square = jnp.mean(values * values, axis=-1, keepdims=True)
    return values * lax.rsqrt(mean_square + EPSILON) * gain


def rope_tables(length):
    lane = jnp.arange(LANES, dtype=jnp.int32)
    half = HD // 2
    freq = jnp.power(ROPE_BASE, -2.0 * (lane % half).astype(F32) / HD)
    angle = jnp.arange(length, dtype=jnp.int32).astype(F32)[:, None] * freq
    sign = jnp.where(lane % HD < half, -1.0, 1.0).astype(F32)
    return jnp.cos(angle), jnp.sin(angle) * sign


def rotate(values, cosine, sine):
    lane = lax.broadcasted_iota(jnp.int32, values.shape, 1)
    swapped = jnp.where(
        lane % HD < HD // 2,
        pltpu.roll(values, LANES - HD // 2, 1),
        pltpu.roll(values, HD // 2, 1),
    )
    return values * cosine + swapped * sine


def dot(a, b):
    return jnp.dot(a, b, preferred_element_type=F32)


def pack_kernel(order, table, prior, cache_k, cache_v, *outs):
    for step, out in enumerate(outs):
        source = order[step]
        for page in range(MAXP):
            at = table[source * MAXP + page]
            out[page * PAGE : (page + 1) * PAGE, :] = cache_k[at]
            out[CONTEXT + page * PAGE : CONTEXT + (page + 1) * PAGE, :] = cache_v[at]
        out[2 * CONTEXT :, :] = jnp.full((INFO, LANES), prior[source].astype(F32), F32).astype(BF)


def pack_pages(order, table, prior, cache_k, cache_v):
    peers = order.shape[0]
    block = jax.ShapeDtypeStruct((2 * CONTEXT + INFO, LANES), BF)
    return pl.pallas_call(
        pack_kernel,
        out_shape=[block] * peers,
        in_specs=[SMEM, SMEM, SMEM, VMEM, VMEM],
        out_specs=[VMEM] * peers,
        name="pack_pages",
    )(order, table, prior, cache_k, cache_v)


def attention_kernel(
    order, starts, counts, priors, group, query, key, value, pages, cosines, sines, mixed, sent, total
):
    step = pl.program_id(0)
    owner = order[step]
    start, count, prior = starts[owner], counts[owner], priors[step]
    rows, qcols = query.shape
    pair = sent.shape[1]

    @pl.when(step == 0)
    def _():
        total[...] = jnp.zeros_like(total)

    @pl.when(count == 0)
    def _():
        sent[...] = jnp.zeros_like(sent)

    @pl.when(count > 0)
    def _():
        slot = lax.broadcasted_iota(jnp.int32, (pair, rows), 0)
        row = lax.broadcasted_iota(jnp.int32, (pair, rows), 1)
        pick = jnp.where((row == slot + start) & (slot < count), 1.0, 0.0).astype(BF)
        cosine = cosines[pl.ds(prior, pair), :]
        sine = sines[pl.ds(prior, pair), :]
        new_key = rotate(dot(pick, key[...]), cosine, sine).astype(BF)
        new_value = dot(pick, value[...]).astype(BF)
        sent[0, :, :LANES] = new_key
        sent[0, :, LANES:] = new_value

        place = lax.broadcasted_iota(jnp.int32, (CONTEXT, pair), 0)
        new_slot = lax.broadcasted_iota(jnp.int32, (CONTEXT, pair), 1)
        put = jnp.where((place == new_slot + prior) & (new_slot < count), 1.0, 0.0).astype(BF)
        position = lax.broadcasted_iota(jnp.int32, (CONTEXT, LANES), 0)
        lane = lax.broadcasted_iota(jnp.int32, (CONTEXT, LANES), 1)
        low = lane < HD

        def merged(new, old):
            whole = jnp.where(position < prior, old.astype(F32), dot(put, new))
            turned = pltpu.roll(whole, HD, 1)
            return (
                jnp.where(low, whole, turned).astype(BF),
                jnp.where(low, turned, whole).astype(BF),
            )

        keys = merged(new_key, pages[0, :CONTEXT, :])
        values = merged(new_value, pages[0, CONTEXT : 2 * CONTEXT, :])

        queries = dot(pick, query[...])
        query_slot = lax.broadcasted_iota(jnp.int32, (2 * pair, CONTEXT), 0)
        query_slot = jnp.where(query_slot >= pair, query_slot - pair, query_slot)
        at = lax.broadcasted_iota(jnp.int32, (2 * pair, CONTEXT), 1)
        allowed = at <= query_slot + prior
        left = lax.broadcasted_iota(jnp.int32, (pair, LANES), 1) < HD
        tiles = qcols // LANES
        outs = []
        for tile in range(tiles):
            kv = tile * 2 // tiles
            turned = rotate(queries[:, tile * LANES : (tile + 1) * LANES], cosine, sine)
            both = jnp.concatenate([jnp.where(left, turned, 0.0), jnp.where(left, 0.0, turned)], 0)
            score = lax.dot_general(
                both.astype(BF), keys[kv], (((1,), (1,)), ((), ())), preferred_element_type=F32
            )
            score = jnp.where(allowed, score * SCORE_MULT, -1e30)
            weight = jnp.exp(score - jnp.max(score, axis=-1, keepdims=True))
            probs = (weight / jnp.sum(weight, axis=-1, keepdims=True)).astype(BF)
            out = dot(probs, values[kv])
            outs.append(jnp.where(left, out[:pair], out[pair:]).astype(BF))
        block = jnp.concatenate(outs, axis=1)
        home = lax.broadcasted_iota(jnp.int32, (rows, pair), 0)
        slot_back = lax.broadcasted_iota(jnp.int32, (rows, pair), 1)
        back = jnp.where((home == slot_back + start) & (slot_back < count), 1.0, 0.0).astype(BF)
        total[...] += dot(back, block)

    @pl.when(step == pl.num_programs(0) - 1)
    def _():
        parts = mixed.shape[0]
        quarter = rows // parts
        for part in range(parts):
            first = pl.multiple_of((group[0] ^ part) * quarter, quarter)
            mixed[part] = total[pl.ds(first, quarter), :].astype(BF)


def attend(order, starts, counts, priors, group, query, key, value, pages, cosines, sines, pair, parts):
    peers = order.shape[0]
    rows, qcols = query.shape
    whole = lambda step, *_: (0, 0)
    here = lambda step, *_: (step, 0, 0)
    return pl.pallas_call(
        attention_kernel,
        out_shape=[
            jax.ShapeDtypeStruct((parts, rows // parts, qcols), BF),
            jax.ShapeDtypeStruct((peers, pair, 2 * LANES), BF),
        ],
        grid_spec=pltpu.PrefetchScalarGridSpec(
            num_scalar_prefetch=5,
            grid=(peers,),
            in_specs=[
                pl.BlockSpec((rows, qcols), whole),
                pl.BlockSpec((rows, LANES), whole),
                pl.BlockSpec((rows, LANES), whole),
                pl.BlockSpec((1,) + pages.shape[1:], here),
                pl.BlockSpec(cosines.shape, whole),
                pl.BlockSpec(sines.shape, whole),
            ],
            out_specs=[
                pl.BlockSpec((parts, rows // parts, qcols), lambda step, *_: (0, 0, 0)),
                pl.BlockSpec((1, pair, 2 * LANES), lambda step, order, *_: (order[step], 0, 0)),
            ],
            scratch_shapes=[pltpu.VMEM((rows, qcols), F32)],
        ),
        compiler_params=pltpu.CompilerParams(
            vmem_limit_bytes=32 * 1024 * 1024, dimension_semantics=("arbitrary",)
        ),
        name="attend",
    )(order, starts, counts, priors, group, query, key, value, pages, cosines, sines)


def store_kernel(table, priors, counts, new, cache_k, cache_v, keys_out, values_out):
    peers, pair, _ = new.shape
    keys_out[...] = cache_k[...]
    values_out[...] = cache_v[...]

    def request(source, carry):
        prior, count = priors[source], counts[source]
        place = lax.broadcasted_iota(jnp.int32, (CONTEXT, pair), 0)
        slot = lax.broadcasted_iota(jnp.int32, (CONTEXT, pair), 1)
        put = jnp.where((place == slot + prior) & (slot < count), 1.0, 0.0).astype(BF)
        moved = dot(put, new[source])
        position = lax.broadcasted_iota(jnp.int32, (PAGE, LANES), 0)
        for page in range(MAXP):
            at = table[source * MAXP + page]
            here = position + page * PAGE
            fresh = (here >= prior) & (here < prior + count)
            rows = moved[page * PAGE : (page + 1) * PAGE]
            keys_out[at] = jnp.where(fresh, rows[:, :LANES], cache_k[at].astype(F32)).astype(BF)
            values_out[at] = jnp.where(fresh, rows[:, LANES:], cache_v[at].astype(F32)).astype(BF)
        return carry

    lax.fori_loop(0, peers, request, 0)


def store_new(table, priors, counts, new, cache_k, cache_v):
    return pl.pallas_call(
        store_kernel,
        out_shape=[jax.ShapeDtypeStruct(cache_k.shape, BF)] * 2,
        in_specs=[SMEM, SMEM, SMEM, VMEM, VMEM, VMEM],
        out_specs=[VMEM] * 2,
        compiler_params=pltpu.CompilerParams(vmem_limit_bytes=32 * 1024 * 1024),
        name="store_new",
    )(table, priors, counts, new, cache_k, cache_v)


def swap(values, axis, size, bit):
    return lax.ppermute(values, axis, [(at, at ^ bit) for at in range(size)])


def feed_forward(rows, w_gate, w_up, w_down):
    gate = dot(rows, w_gate)
    upper = dot(rows, w_up)
    hidden = (jax.nn.silu(gate) * upper).astype(BF)
    return dot(hidden, w_down).astype(BF)


def exchange_mlp(own, peers, w_gate, w_up, w_down):
    send = functools.partial(swap, axis="req", size=peers)
    unit = own.shape[0]
    if peers != 8:
        piece = lax.all_gather(own, "req", axis=0, tiled=True)
        part = feed_forward(piece, w_gate, w_up, w_down)
        return lax.psum_scatter(part, "req", scatter_dimension=0, tiled=True).astype(F32)
    far = send(own, bit=4)
    near = send(own, bit=2)
    side = send(own, bit=1)
    both = send(far, bit=2)
    mine = [own, near, far, both]
    theirs = [side] + [send(rows, bit=1) for rows in mine[1:]]
    sums = []
    for a, b in zip(mine, theirs):
        part = feed_forward(jnp.concatenate([a, b], 0), w_gate, w_up, w_down)
        back = send(part[unit:], bit=1)
        sums.append(part[:unit].astype(F32) + back.astype(F32))
    from_both = send(sums[3].astype(BF), bit=2)
    from_far = send((sums[2] + from_both.astype(F32)).astype(BF), bit=4)
    from_near = send(sums[1].astype(BF), bit=2)
    return sums[0] + from_near.astype(F32) + from_far.astype(F32)


def body(
    hidden_in,
    attn_gain,
    mlp_gain,
    w_query,
    w_key,
    w_value,
    w_out,
    w_gate,
    w_up,
    w_down,
    cache_k,
    cache_v,
    owner_of_row,
    new_len,
    prior_len,
    page_table,
):
    peers = lax.axis_size("req")
    groups = lax.axis_size("grp")
    row_count = hidden_in.shape[0]
    pair = 2 * row_count // peers
    quarter = row_count // groups
    me = lax.axis_index("req")
    group_index = lax.axis_index("grp")
    owners = jnp.arange(peers, dtype=jnp.int32)
    order = owners ^ me if peers == 8 else owners

    packed = pack_pages(order, page_table[0], prior_len[0], cache_k, cache_v)
    if peers == 8:
        pages = [packed[0]] + [swap(packed[bit], "req", peers, bit) for bit in range(1, peers)]
        pages = jnp.stack(pages)
    else:
        pages = lax.all_to_all(jnp.stack(packed), "req", split_axis=0, concat_axis=0, tiled=True)
    priors = pages[:, 2 * CONTEXT, 0].astype(jnp.int32)

    member = owner_of_row[None, :] == owners[:, None]
    counts = jnp.sum(member.astype(jnp.int32), axis=1)
    row_ids = jnp.arange(row_count, dtype=jnp.int32)
    starts = jnp.min(jnp.where(member, row_ids[None, :], row_count), axis=1)
    cosines, sines = rope_tables(CONTEXT + pair)

    normed = normalize(hidden_in.astype(F32), attn_gain).astype(BF)
    query = dot(normed, w_query).astype(BF)
    key = dot(normed, w_key).astype(BF)
    value = dot(normed, w_value).astype(BF)
    mixed, sent = attend(
        order,
        starts,
        counts,
        priors,
        group_index.reshape(1),
        query,
        key,
        value,
        pages,
        cosines,
        sines,
        pair,
        groups,
    )
    new = lax.all_to_all(sent, "req", split_axis=0, concat_axis=0, tiled=True)
    keys_out, values_out = store_new(page_table[0], prior_len[0], new_len[0], new, cache_k, cache_v)

    out_of = lambda part: dot(mixed[part], w_out).astype(BF)
    cross = swap(out_of(3), "grp", groups, 1)
    beside = swap(out_of(1), "grp", groups, 1)
    over = swap((out_of(2).astype(F32) + cross.astype(F32)).astype(BF), "grp", groups, 2)
    attn_sum = out_of(0).astype(F32) + beside.astype(F32) + over.astype(F32)

    own_rows = lax.dynamic_slice_in_dim(hidden_in, group_index * quarter, quarter, 0).astype(F32)
    residual = own_rows + RESIDUAL_MULT * attn_sum
    mlp_in = normalize(residual, mlp_gain).astype(BF)
    down = exchange_mlp(mlp_in, peers, w_gate, w_up, w_down)
    layer_out = (residual + RESIDUAL_MULT * down).astype(BF)
    return (layer_out, keys_out, values_out)


def solution(mesh):
    in_specs = (
        P("req", None),
        P(),
        P(),
        P(None, "grp"),
        P(None, "grp"),
        P(None, "grp"),
        P("grp", None),
        P(None, "req"),
        P(None, "req"),
        P("req", None),
        P("req", None, "grp"),
        P("req", None, "grp"),
        P("req"),
        P("req", None),
        P("req", None),
        P("req", None),
    )
    out_specs = (P(("req", "grp"), None), P("req", None, "grp"), P("req", None, "grp"))
    return jax.shard_map(body, mesh=mesh, in_specs=in_specs, out_specs=out_specs, check_vma=False)
```

```python
import functools

import jax
import jax.numpy as jnp
from jax import lax
from jax.experimental import pallas as pl
from jax.experimental.pallas import tpu as pltpu
from jax.sharding import PartitionSpec as P

HD = 64
PAGE = 16
MAXP = 16
CONTEXT = 256
LANES = 128
INFO = 16


EPSILON = 1e-05
RESIDUAL_MULT = 0.22
SCORE_MULT = 0.015625
ROPE_BASE = 10000000.0
LOG2E = 1.4426950408889634
BF = jnp.bfloat16
F32 = jnp.float32
SMEM = pl.BlockSpec(memory_space=pltpu.SMEM)
VMEM = pl.BlockSpec(memory_space=pltpu.VMEM)
SMALL = pl.CostEstimate(flops=0, bytes_accessed=0, transcendentals=0)


def normalize(values, gain):
    mean_square = jnp.mean(values * values, axis=-1, keepdims=True)
    return values * lax.rsqrt(mean_square + EPSILON) * gain


def rope_tables(length):
    lane = jnp.arange(LANES, dtype=jnp.int32)
    half = HD // 2
    freq = jnp.power(ROPE_BASE, -2.0 * (lane % half).astype(F32) / HD)
    angle = jnp.arange(length, dtype=jnp.int32).astype(F32)[:, None] * freq
    sign = jnp.where(lane % HD < half, -1.0, 1.0).astype(F32)
    return jnp.cos(angle), jnp.sin(angle) * sign


def rotate(values, cosine, sine):
    lane = lax.broadcasted_iota(jnp.int32, values.shape, 1)
    swapped = jnp.where(
        lane % HD < HD // 2,
        pltpu.roll(values, LANES - HD // 2, 1),
        pltpu.roll(values, HD // 2, 1),
    )
    return values * cosine + swapped * sine


def dot(a, b):
    return jnp.dot(a, b, preferred_element_type=F32)


def pack_kernel(table, prior, cache_k, cache_v, out):
    for source in range(out.shape[0]):
        for page in range(MAXP):
            at = table[source * MAXP + page]
            out[source, page * PAGE : (page + 1) * PAGE, :] = cache_k[at]
            out[source, CONTEXT + page * PAGE : CONTEXT + (page + 1) * PAGE, :] = cache_v[at]
        info = jnp.full((INFO, LANES), prior[source].astype(F32), F32)
        out[source, 2 * CONTEXT :, :] = info.astype(BF)


def pack_pages(table, prior, cache_k, cache_v):
    peers = prior.shape[0]
    return pl.pallas_call(
        pack_kernel,
        out_shape=jax.ShapeDtypeStruct((peers, 2 * CONTEXT + INFO, LANES), BF),
        in_specs=[SMEM, SMEM, VMEM, VMEM],
        out_specs=VMEM,
        compiler_params=pltpu.CompilerParams(vmem_limit_bytes=60 * 1024 * 1024),
        name="pack_pages",
        cost_estimate=SMALL,
    )(table, prior, cache_k, cache_v)


def one_hot(shape, start, count, slot_axis):
    slot = lax.broadcasted_iota(jnp.int32, shape, slot_axis)
    row = lax.broadcasted_iota(jnp.int32, shape, 1 - slot_axis)
    return jnp.where((row == slot + start) & (slot < count), 1.0, 0.0).astype(BF)


def project_kernel(starts, counts, hidden, gain, w_query, w_key, w_value, queries, news, whole):
    step = pl.program_id(0)
    rows = hidden.shape[0]
    qcols = w_query.shape[1]
    peers, pair, _ = queries.shape
    normed = normalize(hidden[...].astype(F32), gain[...]).astype(BF)
    here = pl.ds(pl.multiple_of(step * rows, rows), rows)
    whole[here, :qcols] = dot(normed, w_query[...]).astype(BF)
    whole[here, qcols : qcols + LANES] = dot(normed, w_key[...]).astype(BF)
    whole[here, qcols + LANES :] = dot(normed, w_value[...]).astype(BF)

    @pl.when(step == pl.num_programs(0) - 1)
    def _():
        def request(owner, carry):
            pick = one_hot((pair, whole.shape[0]), starts[owner], counts[owner], 0)
            slots = dot(pick, whole[...]).astype(BF)
            queries[owner] = slots[:, :qcols]
            news[owner] = slots[:, qcols:]
            return carry

        lax.fori_loop(0, peers, request, 0)


def project(starts, counts, hidden, gain, w_query, w_key, w_value, pair):
    rows, width = hidden.shape
    peers = starts.shape[0]
    qcols = w_query.shape[1]
    steps = 2
    whole = lambda step, *_: (0, 0)
    every = lambda step, *_: (0, 0, 0)
    return pl.pallas_call(
        project_kernel,
        out_shape=[
            jax.ShapeDtypeStruct((peers, pair, qcols), BF),
            jax.ShapeDtypeStruct((peers, pair, 2 * LANES), BF),
        ],
        grid_spec=pltpu.PrefetchScalarGridSpec(
            num_scalar_prefetch=2,
            grid=(steps,),
            in_specs=[
                pl.BlockSpec((rows // steps, width), lambda step, *_: (step, 0)),
                pl.BlockSpec((1, width), whole),
                pl.BlockSpec(w_query.shape, whole),
                pl.BlockSpec(w_key.shape, whole),
                pl.BlockSpec(w_value.shape, whole),
            ],
            out_specs=[
                pl.BlockSpec((peers, pair, qcols), every),
                pl.BlockSpec((peers, pair, 2 * LANES), every),
            ],
            scratch_shapes=[pltpu.VMEM((rows, qcols + 2 * LANES), BF)],
        ),
        compiler_params=pltpu.CompilerParams(
            vmem_limit_bytes=32 * 1024 * 1024, dimension_semantics=("arbitrary",)
        ),
        name="project",
        cost_estimate=SMALL,
    )(starts, counts, hidden, gain.reshape(1, width), w_query, w_key, w_value)


def attention_kernel(
    starts, counts, group, query, new, pages, cosines, sines, mixed, total
):
    step = pl.program_id(0)
    start, count = starts[step], counts[step]
    _, pair, qcols = query.shape
    rows = total.shape[0]
    parts = mixed.shape[0]
    quarter = rows // parts

    def span(part):
        return pl.ds(pl.multiple_of((group[0] ^ part) * quarter, quarter), quarter)

    @pl.when(step == 0)
    def _():
        total[...] = jnp.zeros_like(total)

    @pl.when(count > 0)
    def _():
        info = pages[0, 2 * CONTEXT :, :].astype(F32)
        prior = jnp.max(info).astype(jnp.int32)
        cosine = cosines[pl.ds(prior, pair), :]
        sine = sines[pl.ds(prior, pair), :]
        new_key = rotate(new[0, :, :LANES].astype(F32), cosine, sine).astype(BF)
        new_value = new[0, :, LANES:]

        place = lax.broadcasted_iota(jnp.int32, (CONTEXT, pair), 0)
        new_slot = lax.broadcasted_iota(jnp.int32, (CONTEXT, pair), 1)
        put = jnp.where((place == new_slot + prior) & (new_slot < count), 1.0, 0.0).astype(BF)
        position = lax.broadcasted_iota(jnp.int32, (CONTEXT, LANES), 0)
        lane = lax.broadcasted_iota(jnp.int32, (CONTEXT, LANES), 1)
        low = lane < HD

        def merged(fresh, old):
            whole = jnp.where(position < prior, old.astype(F32), dot(put, fresh))
            turned = pltpu.roll(whole, HD, 1)
            return (
                jnp.where(low, whole, turned).astype(BF),
                jnp.where(low, turned, whole).astype(BF),
            )

        keys = merged(new_key, pages[0, :CONTEXT, :])
        values = merged(new_value, pages[0, CONTEXT : 2 * CONTEXT, :])

        query_slot = lax.broadcasted_iota(jnp.int32, (2 * pair, CONTEXT), 0)
        query_slot = jnp.where(query_slot >= pair, query_slot - pair, query_slot)
        at = lax.broadcasted_iota(jnp.int32, (2 * pair, CONTEXT), 1)
        allowed = at <= query_slot + prior
        left = lax.broadcasted_iota(jnp.int32, (pair, LANES), 1) < HD
        tiles = qcols // LANES
        outs = []
        for tile in range(tiles):
            kv = tile * 2 // tiles
            turned = rotate(query[0, :, tile * LANES : (tile + 1) * LANES].astype(F32), cosine, sine)
            both = jnp.concatenate([jnp.where(left, turned, 0.0), jnp.where(left, 0.0, turned)], 0)
            score = lax.dot_general(
                both.astype(BF), keys[kv], (((1,), (1,)), ((), ())), preferred_element_type=F32
            )
            score = jnp.where(allowed, score, -1e30)
            score = score - jnp.max(score, axis=-1, keepdims=True)
            weight = jnp.exp2(score * (SCORE_MULT * LOG2E))
            share = 1.0 / jnp.sum(weight, axis=-1, keepdims=True)
            probs = (weight * share).astype(BF)
            out = dot(probs, values[kv])
            outs.append(jnp.where(left, out[:pair], out[pair:]).astype(BF))
        block = jnp.concatenate(outs, axis=1)
        total[...] += dot(one_hot((rows, pair), start, count, 1), block)

    @pl.when(step == pl.num_programs(0) - 1)
    def _():
        for part in range(parts):
            mixed[part] = total[span(part), :].astype(BF)


def attend(starts, counts, group, query, new, pages, cosines, sines, rows, parts):
    peers, pair, qcols = query.shape
    whole = lambda step, *_: (0, 0)
    here = lambda step, *_: (step, 0, 0)
    result = (parts, rows // parts, qcols)
    return pl.pallas_call(
        attention_kernel,
        out_shape=jax.ShapeDtypeStruct(result, BF),
        grid_spec=pltpu.PrefetchScalarGridSpec(
            num_scalar_prefetch=3,
            grid=(peers,),
            in_specs=[
                pl.BlockSpec((1, pair, qcols), here),
                pl.BlockSpec((1, pair, 2 * LANES), here),
                pl.BlockSpec((1,) + pages.shape[1:], here),
                pl.BlockSpec(cosines.shape, whole),
                pl.BlockSpec(sines.shape, whole),
            ],
            out_specs=pl.BlockSpec(result, lambda step, *_: (0, 0, 0)),
            scratch_shapes=[pltpu.VMEM((rows, qcols), F32)],
        ),
        compiler_params=pltpu.CompilerParams(
            vmem_limit_bytes=32 * 1024 * 1024, dimension_semantics=("arbitrary",)
        ),
        name="attend",
        cost_estimate=SMALL,
    )(starts, counts, group, query, new, pages, cosines, sines)


def store_kernel(
    table, priors, counts, new, cosines, sines, cache_k, cache_v, keys_out, values_out
):
    peers, pair, _ = new.shape
    keys_out[...] = cache_k[...]
    values_out[...] = cache_v[...]

    def request(source, carry):
        prior, count = priors[source], counts[source]
        place = lax.broadcasted_iota(jnp.int32, (CONTEXT, pair), 0)
        slot = lax.broadcasted_iota(jnp.int32, (CONTEXT, pair), 1)
        put = jnp.where((place == slot + prior) & (slot < count), 1.0, 0.0).astype(BF)
        cosine = cosines[pl.ds(prior, pair), :]
        sine = sines[pl.ds(prior, pair), :]
        new_key = rotate(new[source, :, :LANES].astype(F32), cosine, sine).astype(BF)
        moved = dot(put, jnp.concatenate([new_key, new[source, :, LANES:]], axis=1))
        position = lax.broadcasted_iota(jnp.int32, (PAGE, LANES), 0)
        for page in range(MAXP):
            at = table[source * MAXP + page]
            here = position + page * PAGE
            fresh = (here >= prior) & (here < prior + count)
            rows = moved[page * PAGE : (page + 1) * PAGE]
            keys_out[at] = jnp.where(fresh, rows[:, :LANES], cache_k[at].astype(F32)).astype(BF)
            values_out[at] = jnp.where(fresh, rows[:, LANES:], cache_v[at].astype(F32)).astype(BF)
        return carry

    lax.fori_loop(0, peers, request, 0)


def store_new(table, priors, counts, new, cosines, sines, cache_k, cache_v):
    return pl.pallas_call(
        store_kernel,
        out_shape=[jax.ShapeDtypeStruct(cache_k.shape, BF)] * 2,
        in_specs=[SMEM] * 3 + [VMEM] * 5,
        out_specs=[VMEM] * 2,
        compiler_params=pltpu.CompilerParams(vmem_limit_bytes=32 * 1024 * 1024),
        name="store_new",
        cost_estimate=SMALL,
    )(table, priors, counts, new, cosines, sines, cache_k, cache_v)


def swap(values, axis, size, bit):
    return lax.ppermute(values, axis, [(at, at ^ bit) for at in range(size)])


def feed_forward(rows, w_gate, w_up, w_down):
    gate = dot(rows, w_gate)
    upper = dot(rows, w_up)
    hidden = (jax.nn.silu(gate) * upper).astype(BF)
    return dot(hidden, w_down).astype(BF)


UNIT_TILE = 256
COLUMN_TILE = 512
HBM = pl.BlockSpec(memory_space=pltpu.HBM)
ROOM = pltpu.CompilerParams(vmem_limit_bytes=16 * 1024 * 1024)


def up_kernel(mine, theirs, gate, upper, mine_out, theirs_out, stack, sems):
    unit = mine.shape[0]
    copies = [
        pltpu.make_async_copy(ref, stack.at[pl.ds(at * unit, unit)], sems.at[at])
        for at, ref in enumerate((mine, theirs))
    ]
    for copy in copies:
        copy.start()
    for copy in copies:
        copy.wait()

    def work(tile, carry):
        span = pl.ds(pl.multiple_of(tile * UNIT_TILE, UNIT_TILE), UNIT_TILE)
        both = dot(stack[...], jnp.concatenate([gate[:, span], upper[:, span]], axis=1))
        hidden = (jax.nn.silu(both[:, :UNIT_TILE]) * both[:, UNIT_TILE:]).astype(BF)
        mine_out[:, span] = hidden[:unit]
        theirs_out[:, span] = hidden[unit:]
        return carry

    lax.fori_loop(0, gate.shape[1] // UNIT_TILE, work, 0)


def mlp_up(mine, theirs, gate, upper):
    unit, width = mine.shape
    return pl.pallas_call(
        up_kernel,
        out_shape=[jax.ShapeDtypeStruct((unit, gate.shape[1]), BF)] * 2,
        in_specs=[HBM, HBM, VMEM, VMEM],
        out_specs=[VMEM] * 2,
        scratch_shapes=[pltpu.VMEM((2 * unit, width), BF), pltpu.SemaphoreType.DMA((2,))],
        compiler_params=ROOM,
        cost_estimate=SMALL,
        name="mlp_up",
    )(mine, theirs, gate, upper)


def down_kernel(count, group, *refs):
    hidden, side, down = refs[:3]
    pieces, outs, stack = refs[3 : 3 + count], refs[3 + count : -1], refs[-1]
    units = hidden.shape[1]
    size = units // count
    stack[:, :units] = hidden[...]
    for at in range(count):
        start = pl.multiple_of((group[0] ^ at) * size, size)
        stack[:, units + at * size : units + (at + 1) * size] = side[:, pl.ds(start, size)]

    def work(tile, carry):
        span = pl.ds(pl.multiple_of(tile * COLUMN_TILE, COLUMN_TILE), COLUMN_TILE)
        weights = jnp.concatenate([down[:, span]] + [ref[:, span] for ref in pieces], axis=0)
        total = dot(stack[...], weights).astype(BF)
        at = 0
        for ref in outs:
            ref[:, span] = total[at : at + ref.shape[0]]
            at += ref.shape[0]
        return carry

    lax.fori_loop(0, down.shape[1] // COLUMN_TILE, work, 0)


def mlp_down(group, hidden, side, down, pieces, sizes):
    many, units = hidden.shape
    width = down.shape[1]
    return pl.pallas_call(
        functools.partial(down_kernel, len(pieces)),
        out_shape=[jax.ShapeDtypeStruct((size, width), BF) for size in sizes],
        in_specs=[SMEM] + [VMEM] * (3 + len(pieces)),
        out_specs=[VMEM] * len(sizes),
        scratch_shapes=[pltpu.VMEM((many, 2 * units), BF)],
        compiler_params=ROOM,
        cost_estimate=SMALL,
        name="mlp_down",
    )(group, hidden, side, down, *pieces)


def after(value, *others):
    return lax.optimization_barrier((value,) + others)[0]


def rows_of(w, index, count):
    size = w.shape[0] // count
    return lax.dynamic_slice_in_dim(w, index * size, size, 0)


def sync(*values):
    return lax.optimization_barrier(values)


def exchange_mlp(own, new, peers, groups, group, held, side_down):
    send = functools.partial(swap, axis="req", size=peers)
    cross = functools.partial(swap, axis="grp", size=groups, bit=1)
    over = functools.partial(swap, axis="grp", size=groups, bit=2)
    add = lambda *terms: sum(term.astype(F32) for term in terms)
    join = lambda *blocks: jnp.concatenate(blocks, axis=0)
    up = lambda mine, theirs: mlp_up(mine, theirs, held[0], held[1])
    unit = own.shape[0]
    half = unit // 2
    own_a, own_b = own[:half], own[half:]

    far_a = send(own_a, bit=4)
    near = send(own, bit=2)
    side_own = send(own, bit=1)
    far_a, near, side_own = sync(far_a, near, side_own)
    far_b = send(after(own_b, far_a), bit=4)
    both_a = send(far_a, bit=2)
    side_near = send(near, bit=1)
    over_down = over(after(side_down, far_a))
    hidden_own, theirs_own = up(own, side_own)
    far_b, both_a, side_near, new, _ = sync(far_b, both_a, side_near, new, hidden_own)
    both_b = send(far_b, bit=2)
    rows_a = join(far_a, both_a)
    side_a = send(rows_a, bit=1)
    hidden_near, theirs_near = up(near, side_near)
    both_b, side_a, over_down, _ = sync(both_b, side_a, over_down, hidden_near)
    rows_b = join(far_b, both_b)
    side_b = send(rows_b, bit=1)
    pieces = [side_down, cross(side_down), over_down, cross(over_down)]
    down = lambda hidden, side, sizes: mlp_down(group, hidden, side, held[2], pieces, sizes)
    hidden_a, theirs_a = up(rows_a, side_a)
    side_b, hidden_a, theirs_a = sync(side_b, hidden_a, theirs_a)
    from_a = send(theirs_a, bit=1)
    hidden_b, theirs_b = up(rows_b, side_b)
    from_b = send(theirs_b, bit=1)
    from_a, _ = sync(from_a, hidden_b)
    sum_far_a, sum_both_a = down(hidden_a, from_a, [half, half])
    back_both_a = send(sum_both_a, bit=2)
    from_b, _ = sync(from_b, sum_far_a)
    from_near = send(after(theirs_near, from_b), bit=1)
    sum_far_b, sum_both_b = down(hidden_b, from_b, [half, half])
    back_both_b = send(sum_both_b, bit=2)
    back_both_a, _ = sync(back_both_a, sum_far_b)
    total_a = add(sum_far_a, back_both_a).astype(BF)
    back_far_a = send(total_a, bit=4)
    back_both_b, _ = sync(back_both_b, total_a)
    total_b = add(sum_far_b, back_both_b).astype(BF)
    back_far_b = send(total_b, bit=4)
    from_own = send(after(theirs_own, from_near), bit=1)
    (sum_near,) = down(after(hidden_near, total_a), from_near, [unit])
    back_near = send(sum_near, bit=2)
    (sum_own,) = down(hidden_own, from_own, [unit])
    return new, add(sum_own, back_near, join(back_far_a, back_far_b))


def body(
    hidden_in,
    attn_gain,
    mlp_gain,
    w_query,
    w_key,
    w_value,
    w_out,
    w_gate,
    w_up,
    w_down,
    cache_k,
    cache_v,
    owner_of_row,
    new_len,
    prior_len,
    page_table,
):
    peers = lax.axis_size("req")
    groups = lax.axis_size("grp")
    row_count = hidden_in.shape[0]
    pair = 2 * row_count // peers
    quarter = row_count // groups
    group_index = lax.axis_index("grp")
    owners = jnp.arange(peers, dtype=jnp.int32)

    member = owner_of_row[None, :] == owners[:, None]
    counts = jnp.sum(member.astype(jnp.int32), axis=1)
    row_ids = jnp.arange(row_count, dtype=jnp.int32)
    starts = jnp.min(jnp.where(member, row_ids[None, :], row_count), axis=1)
    cosines, sines = rope_tables(CONTEXT + pair)

    group = group_index.reshape(1)
    packed = pack_pages(page_table[0], prior_len[0], cache_k, cache_v)
    pages = lax.all_to_all(packed, "req", split_axis=0, concat_axis=0, tiled=True)
    query, fresh = project(starts, counts, hidden_in, attn_gain, w_query, w_key, w_value, pair)
    if peers == 8:
        side_down = swap(after(rows_of(w_down, group_index, groups), fresh), "req", peers, 1)
    mixed = attend(
        starts, counts, group, query, fresh, pages, cosines, sines, row_count, groups
    )
    if peers == 8:
        mixed, side_down = sync(mixed, side_down)

    out_of = lambda part: dot(mixed[part], w_out).astype(BF)
    to_home = functools.partial(swap, axis="grp", size=groups)
    cross = to_home(out_of(3), bit=1)
    beside = to_home(out_of(1), bit=1)
    over = (out_of(2).astype(F32) + cross.astype(F32)).astype(BF)
    new = lax.all_to_all(after(fresh, over), "req", split_axis=0, concat_axis=0, tiled=True)
    over = to_home(over, bit=2)
    attn_sum = out_of(0).astype(F32) + beside.astype(F32) + over.astype(F32)
    own_rows = lax.dynamic_slice_in_dim(hidden_in, group_index * quarter, quarter, 0).astype(F32)
    residual = own_rows + RESIDUAL_MULT * attn_sum
    own = normalize(residual, mlp_gain).astype(BF)
    if peers == 8:
        held = [w_gate, w_up, w_down]
        new, down = exchange_mlp(own, new, peers, groups, group, held, side_down)
    else:
        piece = lax.all_gather(own, "req", axis=0, tiled=True)
        part = feed_forward(piece, w_gate, w_up, w_down)
        down = lax.psum_scatter(part, "req", scatter_dimension=0, tiled=True).astype(F32)
    keys_out, values_out = store_new(page_table[0], prior_len[0], new_len[0], new, cosines, sines, cache_k, cache_v)
    layer_out = (residual + RESIDUAL_MULT * down).astype(BF)
    return (layer_out, keys_out, values_out)


def solution(mesh):
    in_specs = (
        P("req", None),
        P(),
        P(),
        P(None, "grp"),
        P(None, "grp"),
        P(None, "grp"),
        P("grp", None),
        P(None, "req"),
        P(None, "req"),
        P("req", None),
        P("req", None, "grp"),
        P("req", None, "grp"),
        P("req"),
        P("req", None),
        P("req", None),
        P("req", None),
    )
    out_specs = (P(("req", "grp"), None), P("req", None, "grp"), P("req", None, "grp"))
    return jax.shard_map(body, mesh=mesh, in_specs=in_specs, out_specs=out_specs, check_vma=False)
```

```python
import functools

import jax
import jax.numpy as jnp
from jax import lax
from jax.experimental import pallas as pl
from jax.experimental.pallas import tpu as pltpu
from jax.sharding import PartitionSpec as P

HD = 64
PAGE = 16
MAXP = 16
CONTEXT = 256
LANES = 128
INFO = 16


EPSILON = 1e-05
RESIDUAL_MULT = 0.22
SCORE_MULT = 0.015625
ROPE_BASE = 10000000.0
LOG2E = 1.4426950408889634
BF = jnp.bfloat16
F32 = jnp.float32
SMEM = pl.BlockSpec(memory_space=pltpu.SMEM)
VMEM = pl.BlockSpec(memory_space=pltpu.VMEM)
HBM = pl.BlockSpec(memory_space=pltpu.HBM)
SMALL = pl.CostEstimate(flops=0, bytes_accessed=0, transcendentals=0)


def normalize(values, gain):
    mean_square = jnp.mean(values * values, axis=-1, keepdims=True)
    return values * lax.rsqrt(mean_square + EPSILON) * gain


def rope_tables(length):
    lane = jnp.arange(LANES, dtype=jnp.int32)
    half = HD // 2
    freq = jnp.power(ROPE_BASE, -2.0 * (lane % half).astype(F32) / HD)
    angle = jnp.arange(length, dtype=jnp.int32).astype(F32)[:, None] * freq
    sign = jnp.where(lane % HD < half, -1.0, 1.0).astype(F32)
    return jnp.cos(angle), jnp.sin(angle) * sign


def rotate(values, cosine, sine):
    lane = lax.broadcasted_iota(jnp.int32, values.shape, 1)
    swapped = jnp.where(
        lane % HD < HD // 2,
        pltpu.roll(values, LANES - HD // 2, 1),
        pltpu.roll(values, HD // 2, 1),
    )
    return values * cosine + swapped * sine


def dot(a, b):
    return jnp.dot(a, b, preferred_element_type=F32)


def pack_kernel(table, prior, cache_k, cache_v, out):
    for source in range(out.shape[0]):
        for page in range(MAXP):
            at = table[source * MAXP + page]
            out[source, page * PAGE : (page + 1) * PAGE, :] = cache_k[at]
            out[source, CONTEXT + page * PAGE : CONTEXT + (page + 1) * PAGE, :] = cache_v[at]
        info = jnp.full((INFO, LANES), prior[source].astype(F32), F32)
        out[source, 2 * CONTEXT :, :] = info.astype(BF)


def pack_pages(table, prior, cache_k, cache_v):
    peers = prior.shape[0]
    return pl.pallas_call(
        pack_kernel,
        out_shape=jax.ShapeDtypeStruct((peers, 2 * CONTEXT + INFO, LANES), BF),
        in_specs=[SMEM, SMEM, VMEM, VMEM],
        out_specs=VMEM,
        compiler_params=pltpu.CompilerParams(vmem_limit_bytes=60 * 1024 * 1024),
        name="pack_pages",
        cost_estimate=SMALL,
    )(table, prior, cache_k, cache_v)


def one_hot(shape, start, count, slot_axis):
    slot = lax.broadcasted_iota(jnp.int32, shape, slot_axis)
    row = lax.broadcasted_iota(jnp.int32, shape, 1 - slot_axis)
    return jnp.where((row == slot + start) & (slot < count), 1.0, 0.0).astype(BF)


def project_kernel(starts, counts, hidden, gain, w_query, w_key, w_value, queries, news, whole):
    step = pl.program_id(0)
    rows = hidden.shape[0]
    qcols = w_query.shape[1]
    peers, pair, _ = queries.shape
    normed = normalize(hidden[...].astype(F32), gain[...]).astype(BF)
    here = pl.ds(pl.multiple_of(step * rows, rows), rows)
    whole[here, :qcols] = dot(normed, w_query[...]).astype(BF)
    whole[here, qcols : qcols + LANES] = dot(normed, w_key[...]).astype(BF)
    whole[here, qcols + LANES :] = dot(normed, w_value[...]).astype(BF)

    @pl.when(step == pl.num_programs(0) - 1)
    def _():
        def request(owner, carry):
            pick = one_hot((pair, whole.shape[0]), starts[owner], counts[owner], 0)
            slots = dot(pick, whole[...]).astype(BF)
            queries[owner] = slots[:, :qcols]
            news[owner] = slots[:, qcols:]
            return carry

        lax.fori_loop(0, peers, request, 0)


def project(starts, counts, hidden, gain, w_query, w_key, w_value, pair):
    rows, width = hidden.shape
    peers = starts.shape[0]
    qcols = w_query.shape[1]
    steps = 2
    whole = lambda step, *_: (0, 0)
    every = lambda step, *_: (0, 0, 0)
    return pl.pallas_call(
        project_kernel,
        out_shape=[
            jax.ShapeDtypeStruct((peers, pair, qcols), BF),
            jax.ShapeDtypeStruct((peers, pair, 2 * LANES), BF),
        ],
        grid_spec=pltpu.PrefetchScalarGridSpec(
            num_scalar_prefetch=2,
            grid=(steps,),
            in_specs=[
                pl.BlockSpec((rows // steps, width), lambda step, *_: (step, 0)),
                pl.BlockSpec((1, width), whole),
                pl.BlockSpec(w_query.shape, whole),
                pl.BlockSpec(w_key.shape, whole),
                pl.BlockSpec(w_value.shape, whole),
            ],
            out_specs=[
                pl.BlockSpec((peers, pair, qcols), every),
                pl.BlockSpec((peers, pair, 2 * LANES), every),
            ],
            scratch_shapes=[pltpu.VMEM((rows, qcols + 2 * LANES), BF)],
        ),
        compiler_params=pltpu.CompilerParams(
            vmem_limit_bytes=32 * 1024 * 1024, dimension_semantics=("arbitrary",)
        ),
        name="project",
        cost_estimate=SMALL,
    )(starts, counts, hidden, gain.reshape(1, width), w_query, w_key, w_value)


def attention_kernel(
    starts, counts, group, query, new, pages, cosines, sines, mixed, total, arrived, queries, news, sems
):
    step = pl.program_id(0)
    start, count = starts[step], counts[step]
    _, pair, qcols = query.shape
    rows = total.shape[1] - pair
    parts = mixed.shape[0]
    quarter = rows // parts

    def span(part):
        return pl.ds(pl.multiple_of((group[0] ^ part) * quarter, quarter), quarter)

    moved = ((query, queries), (new, news), (pages, arrived))

    @pl.when(step == 0)
    def _():
        for at in range(pages.shape[0]):
            for kind, (source, target) in enumerate(moved):
                pltpu.make_async_copy(source.at[at], target.at[at], sems.at[kind, at]).start()
        total[...] = jnp.zeros_like(total)

    for kind, (_, target) in enumerate(moved):
        pltpu.make_async_copy(target.at[step], target.at[step], sems.at[kind, step]).wait()

    def request(size):
        info = arrived[step, 2 * CONTEXT :, :].astype(F32)
        prior = jnp.max(info).astype(jnp.int32)
        cosine = cosines[pl.ds(prior, size), :]
        sine = sines[pl.ds(prior, size), :]
        new_key = rotate(news[step, :size, :LANES].astype(F32), cosine, sine).astype(BF)
        new_value = news[step, :size, LANES:]

        place = lax.broadcasted_iota(jnp.int32, (CONTEXT, size), 0)
        new_slot = lax.broadcasted_iota(jnp.int32, (CONTEXT, size), 1)
        put = jnp.where((place == new_slot + prior) & (new_slot < count), 1.0, 0.0).astype(BF)
        position = lax.broadcasted_iota(jnp.int32, (CONTEXT, LANES), 0)
        lane = lax.broadcasted_iota(jnp.int32, (CONTEXT, LANES), 1)
        low = lane < HD

        def merged(fresh, old):
            whole = jnp.where(position < prior, old.astype(F32), dot(put, fresh))
            turned = pltpu.roll(whole, HD, 1)
            return (
                jnp.where(low, whole, turned).astype(BF),
                jnp.where(low, turned, whole).astype(BF),
            )

        keys = merged(new_key, arrived[step, :CONTEXT, :])
        values = merged(new_value, arrived[step, CONTEXT : 2 * CONTEXT, :])

        query_slot = lax.broadcasted_iota(jnp.int32, (2 * size, CONTEXT), 0)
        query_slot = jnp.where(query_slot >= size, query_slot - size, query_slot)
        at = lax.broadcasted_iota(jnp.int32, (2 * size, CONTEXT), 1)
        allowed = at <= query_slot + prior
        left = lax.broadcasted_iota(jnp.int32, (size, LANES), 1) < HD
        slot = lax.broadcasted_iota(jnp.int32, (size, LANES), 0)
        tiles = qcols // LANES
        for tile in range(tiles):
            kv = tile * 2 // tiles
            span = slice(tile * LANES, (tile + 1) * LANES)
            turned = rotate(queries[step, :size, span].astype(F32), cosine, sine)
            both = jnp.concatenate([jnp.where(left, turned, 0.0), jnp.where(left, 0.0, turned)], 0)
            score = lax.dot_general(
                both.astype(BF), keys[kv], (((1,), (1,)), ((), ())), preferred_element_type=F32
            )
            score = jnp.where(allowed, score, -1e30)
            score = score - jnp.max(score, axis=-1, keepdims=True)
            weight = jnp.exp2(score * (SCORE_MULT * LOG2E))
            share = 1.0 / jnp.sum(weight, axis=-1, keepdims=True)
            probs = (weight * share).astype(BF)
            out = dot(probs, values[kv])
            out = jnp.where(left, out[:size], out[size:])
            rows_here = pl.ds(start, size)
            total[tile, rows_here] = jnp.where(slot < count, out, total[tile, rows_here])

    @pl.when(count > pair // 2)
    def _():
        request(pair)

    @pl.when((count > 0) & (count <= pair // 2))
    def _():
        request(pair // 2)

    @pl.when(step == pl.num_programs(0) - 1)
    def _():
        for part in range(parts):
            for tile in range(qcols // LANES):
                here = slice(tile * LANES, (tile + 1) * LANES)
                mixed[part, :, here] = total[tile, span(part), :].astype(BF)


def attend(starts, counts, group, query, new, pages, cosines, sines, rows, parts):
    peers, pair, qcols = query.shape
    whole = lambda step, *_: (0, 0)
    result = (parts, rows // parts, qcols)
    return pl.pallas_call(
        attention_kernel,
        out_shape=jax.ShapeDtypeStruct(result, BF),
        grid_spec=pltpu.PrefetchScalarGridSpec(
            num_scalar_prefetch=3,
            grid=(peers,),
            in_specs=[
                HBM,
                HBM,
                HBM,
                pl.BlockSpec(cosines.shape, whole),
                pl.BlockSpec(sines.shape, whole),
            ],
            out_specs=pl.BlockSpec(result, lambda step, *_: (0, 0, 0)),
            scratch_shapes=[
                pltpu.VMEM((qcols // LANES, rows + pair, LANES), F32),
                pltpu.VMEM(pages.shape, BF),
                pltpu.VMEM(query.shape, BF),
                pltpu.VMEM(new.shape, BF),
                pltpu.SemaphoreType.DMA((3, peers)),
            ],
        ),
        compiler_params=pltpu.CompilerParams(
            vmem_limit_bytes=60 * 1024 * 1024, dimension_semantics=("arbitrary",)
        ),
        name="attend",
        cost_estimate=SMALL,
    )(starts, counts, group, query, new, pages, cosines, sines)


def store_kernel(
    table, priors, counts, new, cosines, sines, cache_k, cache_v, keys_out, values_out
):
    peers, pair, _ = new.shape
    keys_out[...] = cache_k[...]
    values_out[...] = cache_v[...]

    def request(source, carry):
        prior, count = priors[source], counts[source]
        place = lax.broadcasted_iota(jnp.int32, (CONTEXT, pair), 0)
        slot = lax.broadcasted_iota(jnp.int32, (CONTEXT, pair), 1)
        put = jnp.where((place == slot + prior) & (slot < count), 1.0, 0.0).astype(BF)
        cosine = cosines[pl.ds(prior, pair), :]
        sine = sines[pl.ds(prior, pair), :]
        new_key = rotate(new[source, :, :LANES].astype(F32), cosine, sine).astype(BF)
        moved = dot(put, jnp.concatenate([new_key, new[source, :, LANES:]], axis=1))
        position = lax.broadcasted_iota(jnp.int32, (PAGE, LANES), 0)
        for page in range(MAXP):
            at = table[source * MAXP + page]
            here = position + page * PAGE
            fresh = (here >= prior) & (here < prior + count)
            rows = moved[page * PAGE : (page + 1) * PAGE]
            keys_out[at] = jnp.where(fresh, rows[:, :LANES], cache_k[at].astype(F32)).astype(BF)
            values_out[at] = jnp.where(fresh, rows[:, LANES:], cache_v[at].astype(F32)).astype(BF)
        return carry

    lax.fori_loop(0, peers, request, 0)


def store_new(table, priors, counts, new, cosines, sines, cache_k, cache_v):
    return pl.pallas_call(
        store_kernel,
        out_shape=[jax.ShapeDtypeStruct(cache_k.shape, BF)] * 2,
        in_specs=[SMEM] * 3 + [VMEM] * 5,
        out_specs=[VMEM] * 2,
        compiler_params=pltpu.CompilerParams(vmem_limit_bytes=32 * 1024 * 1024),
        name="store_new",
        cost_estimate=SMALL,
    )(table, priors, counts, new, cosines, sines, cache_k, cache_v)


def swap(values, axis, size, bit):
    return lax.ppermute(values, axis, [(at, at ^ bit) for at in range(size)])


def feed_forward(rows, w_gate, w_up, w_down):
    gate = dot(rows, w_gate)
    upper = dot(rows, w_up)
    hidden = (jax.nn.silu(gate) * upper).astype(BF)
    return dot(hidden, w_down).astype(BF)


def finish_kernel(base, over, gain, residual, own, own_a, own_b, arrived, sem):
    copy = pltpu.make_async_copy(over, arrived, sem)
    copy.start()
    copy.wait()
    half, block = own_a.shape[0], 16
    for at in range(0, own.shape[0], block):
        rows = slice(at, at + block)
        values = base[rows] + RESIDUAL_MULT * arrived[rows].astype(F32)
        residual[rows] = values
        normed = normalize(values, gain[...]).astype(BF)
        own[rows] = normed
        if at < half:
            own_a[rows] = normed
        else:
            own_b[at - half : at - half + block] = normed


def finish(base, over, gain):
    rows, width = base.shape
    shape = lambda count, kind: jax.ShapeDtypeStruct((count, width), kind)
    return pl.pallas_call(
        finish_kernel,
        out_shape=[shape(rows, F32), shape(rows, BF), shape(rows // 2, BF), shape(rows // 2, BF)],
        in_specs=[VMEM, HBM, VMEM],
        out_specs=[VMEM] * 4,
        scratch_shapes=[pltpu.VMEM((rows, width), BF), pltpu.SemaphoreType.DMA],
        compiler_params=pltpu.CompilerParams(vmem_limit_bytes=16 * 1024 * 1024),
        cost_estimate=SMALL,
        name="finish",
    )(base, over, gain.reshape(1, width))


UNIT_TILE = 256
COLUMN_TILE = 512
ROOM = pltpu.CompilerParams(vmem_limit_bytes=16 * 1024 * 1024)


def up_kernel(count, *refs):
    rows, (gate, upper, mine_out, theirs_out, stack, sems) = refs[:count], refs[count:]
    unit = mine_out.shape[0]
    copies, start = [], 0
    for at, ref in enumerate(rows):
        target = stack.at[pl.ds(start, ref.shape[0])]
        copies.append(pltpu.make_async_copy(ref, target, sems.at[at]))
        start += ref.shape[0]
    for copy in copies:
        copy.start()
    for copy in copies:
        copy.wait()

    def work(tile, carry):
        span = pl.ds(pl.multiple_of(tile * UNIT_TILE, UNIT_TILE), UNIT_TILE)
        both = dot(stack[...], jnp.concatenate([gate[:, span], upper[:, span]], axis=1))
        hidden = (jax.nn.silu(both[:, :UNIT_TILE]) * both[:, UNIT_TILE:]).astype(BF)
        mine_out[:, span] = hidden[:unit]
        theirs_out[:, span] = hidden[unit:]
        return carry

    lax.fori_loop(0, gate.shape[1] // UNIT_TILE, work, 0)


def mlp_up(mine, theirs, gate, upper):
    unit, width = sum(ref.shape[0] for ref in mine), gate.shape[0]
    count = len(mine) + len(theirs)
    return pl.pallas_call(
        functools.partial(up_kernel, count),
        out_shape=[jax.ShapeDtypeStruct((unit, gate.shape[1]), BF)] * 2,
        in_specs=[HBM] * count + [VMEM, VMEM],
        out_specs=[VMEM] * 2,
        scratch_shapes=[pltpu.VMEM((2 * unit, width), BF), pltpu.SemaphoreType.DMA((count,))],
        compiler_params=ROOM,
        cost_estimate=SMALL,
        name="mlp_up",
    )(*mine, *theirs, gate, upper)


def down_kernel(count, group, *refs):
    hidden, side, down = refs[:3]
    pieces, outs, stack = refs[3 : 3 + count], refs[3 + count : -1], refs[-1]
    units = hidden.shape[1]
    size = units // count
    stack[:, :units] = hidden[...]
    for at in range(count):
        start = pl.multiple_of((group[0] ^ at) * size, size)
        stack[:, units + at * size : units + (at + 1) * size] = side[:, pl.ds(start, size)]

    def work(tile, carry):
        span = pl.ds(pl.multiple_of(tile * COLUMN_TILE, COLUMN_TILE), COLUMN_TILE)
        weights = jnp.concatenate([down[:, span]] + [ref[:, span] for ref in pieces], axis=0)
        total = dot(stack[...], weights).astype(BF)
        at = 0
        for ref in outs:
            ref[:, span] = total[at : at + ref.shape[0]]
            at += ref.shape[0]
        return carry

    lax.fori_loop(0, down.shape[1] // COLUMN_TILE, work, 0)


def mlp_down(group, hidden, side, down, pieces, sizes):
    many, units = hidden.shape
    width = down.shape[1]
    return pl.pallas_call(
        functools.partial(down_kernel, len(pieces)),
        out_shape=[jax.ShapeDtypeStruct((size, width), BF) for size in sizes],
        in_specs=[SMEM] + [VMEM] * (3 + len(pieces)),
        out_specs=[VMEM] * len(sizes),
        scratch_shapes=[pltpu.VMEM((many, 2 * units), BF)],
        compiler_params=ROOM,
        cost_estimate=SMALL,
        name="mlp_down",
    )(group, hidden, side, down, *pieces)


def after(value, *others):
    return lax.optimization_barrier((value,) + others)[0]


def rows_of(w, index, count):
    size = w.shape[0] // count
    return lax.dynamic_slice_in_dim(w, index * size, size, 0)


def sync(*values):
    return lax.optimization_barrier(values)


def exchange_mlp(own, own_a, own_b, peers, groups, group, held, side_down):
    send = functools.partial(swap, axis="req", size=peers)
    cross = functools.partial(swap, axis="grp", size=groups, bit=1)
    over = functools.partial(swap, axis="grp", size=groups, bit=2)
    add = lambda *terms: sum(term.astype(F32) for term in terms)
    join = lambda *blocks: jnp.concatenate(blocks, axis=0)
    up = lambda mine, theirs: mlp_up(mine, theirs, held[0], held[1])
    unit = own.shape[0]
    half = unit // 2

    far_a = send(own_a, bit=4)
    near_a = send(own_a, bit=2)
    side = send(own, bit=1)
    far_a, near_a, side = sync(far_a, near_a, side)
    far_b = send(after(own_b, far_a), bit=4)
    both_a = send(far_a, bit=2)
    side_far_a = send(far_a, bit=1)
    side_near_a = send(near_a, bit=1)
    over_down = over(after(side_down, own))
    hidden_own, theirs_own = up([own], [side])
    far_b, both_a, side_far_a, side_near_a, _ = sync(
        far_b, both_a, side_far_a, side_near_a, hidden_own
    )
    both_b = send(far_b, bit=2)
    near_b = send(after(own_b, far_b), bit=2)
    side_far_b = send(far_b, bit=1)
    side_both_a = send(both_a, bit=1)
    hidden_a, theirs_a = up([far_a, near_a], [side_far_a, side_near_a])
    both_b, near_b, side_far_b, side_both_a, over_down, _ = sync(
        both_b, near_b, side_far_b, side_both_a, over_down, hidden_a
    )
    side_both_b = send(both_b, bit=1)
    pieces = [side_down, cross(side_down), over_down, cross(over_down)]
    down = lambda hidden, other, sizes: mlp_down(group, hidden, other, held[2], pieces, sizes)
    hidden_b, theirs_b = up([far_b, both_a], [side_far_b, side_both_a])
    from_b = send(theirs_b, bit=1)
    side_both_b, _ = sync(side_both_b, hidden_b)
    side_near_b = send(after(near_b, side_both_b), bit=1)
    hidden_c, theirs_c = up([both_b], [side_both_b])
    from_c = send(theirs_c, bit=1)
    from_b, _ = sync(from_b, hidden_c)
    sum_far_b, sum_both_a = down(hidden_b, from_b, [half, half])
    back_both_a = send(sum_both_a, bit=2)
    from_c, _ = sync(from_c, sum_both_a)
    from_a = send(after(theirs_a, from_c), bit=1)
    (sum_both_b,) = down(hidden_c, from_c, [half])
    back_both_b = send(sum_both_b, bit=2)
    side_near_b, _ = sync(side_near_b, sum_both_b)
    hidden_d, theirs_d = up([near_b], [side_near_b])
    from_d = send(theirs_d, bit=1)
    from_a, back_both_a, _ = sync(from_a, back_both_a, hidden_d)
    sum_far_a, sum_near_a = down(hidden_a, from_a, [half, half])
    total_a = add(sum_far_a, back_both_a).astype(BF)
    back_far_a = send(total_a, bit=4)
    back_near_a = send(sum_near_a, bit=2)
    back_both_b, _ = sync(back_both_b, total_a)
    total_b = add(sum_far_b, back_both_b).astype(BF)
    back_far_b = send(total_b, bit=4)
    from_own = send(after(theirs_own, total_b), bit=1)
    (sum_near_b,) = down(hidden_d, after(from_d, total_b), [half])
    back_near_b = send(sum_near_b, bit=2)
    (sum_own,) = down(hidden_own, after(from_own, sum_near_b), [unit])
    return add(
        sum_own, join(back_near_a, back_near_b), join(back_far_a, back_far_b)
    )


def body(
    hidden_in,
    attn_gain,
    mlp_gain,
    w_query,
    w_key,
    w_value,
    w_out,
    w_gate,
    w_up,
    w_down,
    cache_k,
    cache_v,
    owner_of_row,
    new_len,
    prior_len,
    page_table,
):
    peers = lax.axis_size("req")
    groups = lax.axis_size("grp")
    row_count = hidden_in.shape[0]
    pair = 2 * row_count // peers
    quarter = row_count // groups
    group_index = lax.axis_index("grp")
    owners = jnp.arange(peers, dtype=jnp.int32)

    member = owner_of_row[None, :] == owners[:, None]
    counts = jnp.sum(member.astype(jnp.int32), axis=1)
    row_ids = jnp.arange(row_count, dtype=jnp.int32)
    starts = jnp.min(jnp.where(member, row_ids[None, :], row_count), axis=1)
    cosines, sines = rope_tables(CONTEXT + pair)

    group = group_index.reshape(1)
    packed = pack_pages(page_table[0], prior_len[0], cache_k, cache_v)
    pages = lax.all_to_all(packed, "req", split_axis=0, concat_axis=0, tiled=True)
    query, fresh = project(starts, counts, after(hidden_in, cosines, sines), attn_gain, w_query, w_key, w_value, pair)
    if peers == 8:
        side_down = swap(rows_of(w_down, group_index, groups), "req", peers, 1)
    mixed = attend(
        starts, counts, group, query, fresh, pages, cosines, sines, row_count, groups
    )
    new = lax.all_to_all(after(fresh, pages), "req", split_axis=0, concat_axis=0, tiled=True)
    if peers == 8:
        mixed, side_down, new = sync(mixed, side_down, new)

    out_of = lambda part: dot(part, w_out).astype(BF)
    to_home = functools.partial(swap, axis="grp", size=groups)
    cross = out_of(mixed[3])
    later = after(mixed, cross)
    cross = to_home(cross, bit=1)
    over = (out_of(mixed[2]).astype(F32) + cross.astype(F32)).astype(BF)
    over = to_home(over, bit=2)
    beside = to_home(out_of(later[1]), bit=1)
    own_rows = lax.dynamic_slice_in_dim(hidden_in, group_index * quarter, quarter, 0).astype(F32)
    near_sum = out_of(later[0]).astype(F32) + beside.astype(F32)
    residual, own, own_a, own_b = finish(own_rows + RESIDUAL_MULT * near_sum, over, mlp_gain)
    if peers == 8:
        held = [w_gate, w_up, w_down]
        down = exchange_mlp(own, own_a, own_b, peers, groups, group, held, side_down)
    else:
        piece = lax.all_gather(own, "req", axis=0, tiled=True)
        part = feed_forward(piece, w_gate, w_up, w_down)
        down = lax.psum_scatter(part, "req", scatter_dimension=0, tiled=True).astype(F32)
    keys_out, values_out = store_new(page_table[0], prior_len[0], new_len[0], new, cosines, sines, cache_k, cache_v)
    layer_out = (residual + RESIDUAL_MULT * down).astype(BF)
    return (layer_out, keys_out, values_out)


def solution(mesh):
    in_specs = (
        P("req", None),
        P(),
        P(),
        P(None, "grp"),
        P(None, "grp"),
        P(None, "grp"),
        P("grp", None),
        P(None, "req"),
        P(None, "req"),
        P("req", None),
        P("req", None, "grp"),
        P("req", None, "grp"),
        P("req"),
        P("req", None),
        P("req", None),
        P("req", None),
    )
    out_specs = (P(("req", "grp"), None), P("req", None, "grp"), P("req", None, "grp"))
    return jax.shard_map(body, mesh=mesh, in_specs=in_specs, out_specs=out_specs, check_vma=False)
```

```python
import functools

import jax
import jax.numpy as jnp
from jax import lax
from jax.experimental import pallas as pl
from jax.experimental.pallas import tpu as pltpu
from jax.sharding import PartitionSpec as P

HD = 64
PAGE = 16
MAXP = 16
CONTEXT = 256
LANES = 128
INFO = 16


EPSILON = 1e-05
RESIDUAL_MULT = 0.22
SCORE_MULT = 0.015625
ROPE_BASE = 10000000.0
LOG2E = 1.4426950408889634
BF = jnp.bfloat16
F32 = jnp.float32
SMEM = pl.BlockSpec(memory_space=pltpu.SMEM)
VMEM = pl.BlockSpec(memory_space=pltpu.VMEM)
HBM = pl.BlockSpec(memory_space=pltpu.HBM)
SMALL = pl.CostEstimate(flops=0, bytes_accessed=0, transcendentals=0)


def normalize(values, gain):
    mean_square = jnp.mean(values * values, axis=-1, keepdims=True)
    return values * lax.rsqrt(mean_square + EPSILON) * gain


def rope_tables(length):
    lane = jnp.arange(LANES, dtype=jnp.int32)
    half = HD // 2
    freq = jnp.power(ROPE_BASE, -2.0 * (lane % half).astype(F32) / HD)
    angle = jnp.arange(length, dtype=jnp.int32).astype(F32)[:, None] * freq
    sign = jnp.where(lane % HD < half, -1.0, 1.0).astype(F32)
    return jnp.cos(angle), jnp.sin(angle) * sign


def rotate(values, cosine, sine):
    lane = lax.broadcasted_iota(jnp.int32, values.shape, 1)
    swapped = jnp.where(
        lane % HD < HD // 2,
        pltpu.roll(values, LANES - HD // 2, 1),
        pltpu.roll(values, HD // 2, 1),
    )
    return values * cosine + swapped * sine


def dot(a, b):
    return jnp.dot(a, b, preferred_element_type=F32)


def pack_kernel(table, prior, cache_k, cache_v, out):
    for source in range(out.shape[0]):
        for page in range(MAXP):
            at = table[source * MAXP + page]
            out[source, page * PAGE : (page + 1) * PAGE, :] = cache_k[at]
            out[source, CONTEXT + page * PAGE : CONTEXT + (page + 1) * PAGE, :] = cache_v[at]
        info = jnp.full((INFO, LANES), prior[source].astype(F32), F32)
        out[source, 2 * CONTEXT :, :] = info.astype(BF)


def pack_pages(table, prior, cache_k, cache_v):
    peers = prior.shape[0]
    return pl.pallas_call(
        pack_kernel,
        out_shape=jax.ShapeDtypeStruct((peers, 2 * CONTEXT + INFO, LANES), BF),
        in_specs=[SMEM, SMEM, VMEM, VMEM],
        out_specs=VMEM,
        compiler_params=pltpu.CompilerParams(vmem_limit_bytes=60 * 1024 * 1024),
        name="pack_pages",
        cost_estimate=SMALL,
    )(table, prior, cache_k, cache_v)


def one_hot(shape, start, count, slot_axis):
    slot = lax.broadcasted_iota(jnp.int32, shape, slot_axis)
    row = lax.broadcasted_iota(jnp.int32, shape, 1 - slot_axis)
    return jnp.where((row == slot + start) & (slot < count), 1.0, 0.0).astype(BF)


def project_kernel(starts, counts, hidden, gain, w_query, w_key, w_value, queries, news, whole):
    step = pl.program_id(0)
    rows = hidden.shape[0]
    qcols = w_query.shape[1]
    peers, pair, _ = queries.shape
    normed = normalize(hidden[...].astype(F32), gain[...]).astype(BF)
    here = pl.ds(pl.multiple_of(step * rows, rows), rows)
    whole[here, :qcols] = dot(normed, w_query[...]).astype(BF)
    whole[here, qcols : qcols + LANES] = dot(normed, w_key[...]).astype(BF)
    whole[here, qcols + LANES :] = dot(normed, w_value[...]).astype(BF)

    @pl.when(step == pl.num_programs(0) - 1)
    def _():
        def request(owner, carry):
            pick = one_hot((pair, whole.shape[0]), starts[owner], counts[owner], 0)
            slots = dot(pick, whole[...]).astype(BF)
            queries[owner] = slots[:, :qcols]
            news[owner] = slots[:, qcols:]
            return carry

        lax.fori_loop(0, peers, request, 0)


def project(starts, counts, hidden, gain, w_query, w_key, w_value, pair):
    rows, width = hidden.shape
    peers = starts.shape[0]
    qcols = w_query.shape[1]
    steps = 2
    whole = lambda step, *_: (0, 0)
    every = lambda step, *_: (0, 0, 0)
    return pl.pallas_call(
        project_kernel,
        out_shape=[
            jax.ShapeDtypeStruct((peers, pair, qcols), BF),
            jax.ShapeDtypeStruct((peers, pair, 2 * LANES), BF),
        ],
        grid_spec=pltpu.PrefetchScalarGridSpec(
            num_scalar_prefetch=2,
            grid=(steps,),
            in_specs=[
                pl.BlockSpec((rows // steps, width), lambda step, *_: (step, 0)),
                pl.BlockSpec((1, width), whole),
                pl.BlockSpec(w_query.shape, whole),
                pl.BlockSpec(w_key.shape, whole),
                pl.BlockSpec(w_value.shape, whole),
            ],
            out_specs=[
                pl.BlockSpec((peers, pair, qcols), every),
                pl.BlockSpec((peers, pair, 2 * LANES), every),
            ],
            scratch_shapes=[pltpu.VMEM((rows, qcols + 2 * LANES), BF)],
        ),
        compiler_params=pltpu.CompilerParams(
            vmem_limit_bytes=32 * 1024 * 1024, dimension_semantics=("arbitrary",)
        ),
        name="project",
        cost_estimate=SMALL,
    )(starts, counts, hidden, gain.reshape(1, width), w_query, w_key, w_value)


def attention_kernel(
    starts, counts, group, query, new, pages, cosines, sines, mixed, total, arrived, queries, news, sems
):
    step = pl.program_id(0)
    start, count = starts[step], counts[step]
    _, pair, qcols = query.shape
    rows = total.shape[1] - pair
    parts = mixed.shape[0]
    quarter = rows // parts

    def span(part):
        return pl.ds(pl.multiple_of((group[0] ^ part) * quarter, quarter), quarter)

    moved = ((query, queries), (new, news), (pages, arrived))

    @pl.when(step == 0)
    def _():
        for at in range(pages.shape[0]):
            for kind, (source, target) in enumerate(moved):
                pltpu.make_async_copy(source.at[at], target.at[at], sems.at[kind, at]).start()
        total[...] = jnp.zeros_like(total)

    for kind, (_, target) in enumerate(moved):
        pltpu.make_async_copy(target.at[step], target.at[step], sems.at[kind, step]).wait()

    def request(size):
        info = arrived[step, 2 * CONTEXT :, :].astype(F32)
        prior = jnp.max(info).astype(jnp.int32)
        cosine = cosines[pl.ds(prior, size), :]
        sine = sines[pl.ds(prior, size), :]
        new_key = rotate(news[step, :size, :LANES].astype(F32), cosine, sine).astype(BF)
        new_value = news[step, :size, LANES:]

        place = lax.broadcasted_iota(jnp.int32, (CONTEXT, size), 0)
        new_slot = lax.broadcasted_iota(jnp.int32, (CONTEXT, size), 1)
        put = jnp.where((place == new_slot + prior) & (new_slot < count), 1.0, 0.0).astype(BF)
        position = lax.broadcasted_iota(jnp.int32, (CONTEXT, LANES), 0)
        lane = lax.broadcasted_iota(jnp.int32, (CONTEXT, LANES), 1)
        low = lane < HD

        def merged(fresh, old):
            whole = jnp.where(position < prior, old.astype(F32), dot(put, fresh))
            turned = pltpu.roll(whole, HD, 1)
            return (
                jnp.where(low, whole, turned).astype(BF),
                jnp.where(low, turned, whole).astype(BF),
            )

        keys = merged(new_key, arrived[step, :CONTEXT, :])
        values = merged(new_value, arrived[step, CONTEXT : 2 * CONTEXT, :])

        query_slot = lax.broadcasted_iota(jnp.int32, (2 * size, CONTEXT), 0)
        query_slot = jnp.where(query_slot >= size, query_slot - size, query_slot)
        at = lax.broadcasted_iota(jnp.int32, (2 * size, CONTEXT), 1)
        allowed = at <= query_slot + prior
        left = lax.broadcasted_iota(jnp.int32, (size, LANES), 1) < HD
        slot = lax.broadcasted_iota(jnp.int32, (size, LANES), 0)
        tiles = qcols // LANES
        for tile in range(tiles):
            kv = tile * 2 // tiles
            span = slice(tile * LANES, (tile + 1) * LANES)
            turned = rotate(queries[step, :size, span].astype(F32), cosine, sine)
            both = jnp.concatenate([jnp.where(left, turned, 0.0), jnp.where(left, 0.0, turned)], 0)
            score = lax.dot_general(
                both.astype(BF), keys[kv], (((1,), (1,)), ((), ())), preferred_element_type=F32
            )
            score = jnp.where(allowed, score, -1e30)
            score = score - jnp.max(score, axis=-1, keepdims=True)
            weight = jnp.exp2(score * (SCORE_MULT * LOG2E))
            share = 1.0 / jnp.sum(weight, axis=-1, keepdims=True)
            probs = (weight * share).astype(BF)
            out = dot(probs, values[kv])
            out = jnp.where(left, out[:size], out[size:])
            rows_here = pl.ds(start, size)
            total[tile, rows_here] = jnp.where(slot < count, out, total[tile, rows_here])

    @pl.when(count > pair // 2)
    def _():
        request(pair)

    @pl.when((count > 0) & (count <= pair // 2))
    def _():
        request(pair // 2)

    @pl.when(step == pl.num_programs(0) - 1)
    def _():
        for part in range(parts):
            for tile in range(qcols // LANES):
                here = slice(tile * LANES, (tile + 1) * LANES)
                mixed[part, :, here] = total[tile, span(part), :].astype(BF)


def attend(starts, counts, group, query, new, pages, cosines, sines, rows, parts):
    peers, pair, qcols = query.shape
    whole = lambda step, *_: (0, 0)
    result = (parts, rows // parts, qcols)
    return pl.pallas_call(
        attention_kernel,
        out_shape=jax.ShapeDtypeStruct(result, BF),
        grid_spec=pltpu.PrefetchScalarGridSpec(
            num_scalar_prefetch=3,
            grid=(peers,),
            in_specs=[
                HBM,
                HBM,
                HBM,
                pl.BlockSpec(cosines.shape, whole),
                pl.BlockSpec(sines.shape, whole),
            ],
            out_specs=pl.BlockSpec(result, lambda step, *_: (0, 0, 0)),
            scratch_shapes=[
                pltpu.VMEM((qcols // LANES, rows + pair, LANES), F32),
                pltpu.VMEM(pages.shape, BF),
                pltpu.VMEM(query.shape, BF),
                pltpu.VMEM(new.shape, BF),
                pltpu.SemaphoreType.DMA((3, peers)),
            ],
        ),
        compiler_params=pltpu.CompilerParams(
            vmem_limit_bytes=60 * 1024 * 1024, dimension_semantics=("arbitrary",)
        ),
        name="attend",
        cost_estimate=SMALL,
    )(starts, counts, group, query, new, pages, cosines, sines)


def store_kernel(
    table, priors, counts, new, cosines, sines, cache_k, cache_v, keys_out, values_out
):
    peers, pair, _ = new.shape
    keys_out[...] = cache_k[...]
    values_out[...] = cache_v[...]

    def request(source, carry):
        prior, count = priors[source], counts[source]
        place = lax.broadcasted_iota(jnp.int32, (CONTEXT, pair), 0)
        slot = lax.broadcasted_iota(jnp.int32, (CONTEXT, pair), 1)
        put = jnp.where((place == slot + prior) & (slot < count), 1.0, 0.0).astype(BF)
        cosine = cosines[pl.ds(prior, pair), :]
        sine = sines[pl.ds(prior, pair), :]
        new_key = rotate(new[source, :, :LANES].astype(F32), cosine, sine).astype(BF)
        moved = dot(put, jnp.concatenate([new_key, new[source, :, LANES:]], axis=1))
        position = lax.broadcasted_iota(jnp.int32, (PAGE, LANES), 0)
        for page in range(MAXP):
            at = table[source * MAXP + page]
            here = position + page * PAGE
            fresh = (here >= prior) & (here < prior + count)
            rows = moved[page * PAGE : (page + 1) * PAGE]
            keys_out[at] = jnp.where(fresh, rows[:, :LANES], cache_k[at].astype(F32)).astype(BF)
            values_out[at] = jnp.where(fresh, rows[:, LANES:], cache_v[at].astype(F32)).astype(BF)
        return carry

    lax.fori_loop(0, peers, request, 0)


def store_new(table, priors, counts, new, cosines, sines, cache_k, cache_v):
    return pl.pallas_call(
        store_kernel,
        out_shape=[jax.ShapeDtypeStruct(cache_k.shape, BF)] * 2,
        in_specs=[SMEM] * 3 + [VMEM] * 5,
        out_specs=[VMEM] * 2,
        compiler_params=pltpu.CompilerParams(vmem_limit_bytes=32 * 1024 * 1024),
        name="store_new",
        cost_estimate=SMALL,
    )(table, priors, counts, new, cosines, sines, cache_k, cache_v)


def swap(values, axis, size, bit):
    return lax.ppermute(values, axis, [(at, at ^ bit) for at in range(size)])


def feed_forward(rows, w_gate, w_up, w_down):
    gate = dot(rows, w_gate)
    upper = dot(rows, w_up)
    hidden = (jax.nn.silu(gate) * upper).astype(BF)
    return dot(hidden, w_down).astype(BF)


def finish_kernel(base, over, gain, residual, own, own_a, own_b, arrived, sem):
    copy = pltpu.make_async_copy(over, arrived, sem)
    copy.start()
    copy.wait()
    half, block = own_a.shape[0], 16
    for at in range(0, own.shape[0], block):
        rows = slice(at, at + block)
        values = base[rows] + RESIDUAL_MULT * arrived[rows].astype(F32)
        residual[rows] = values
        normed = normalize(values, gain[...]).astype(BF)
        own[rows] = normed
        if at < half:
            own_a[rows] = normed
        else:
            own_b[at - half : at - half + block] = normed


def finish(base, over, gain):
    rows, width = base.shape
    shape = lambda count, kind: jax.ShapeDtypeStruct((count, width), kind)
    return pl.pallas_call(
        finish_kernel,
        out_shape=[shape(rows, F32), shape(rows, BF), shape(rows // 2, BF), shape(rows // 2, BF)],
        in_specs=[VMEM, HBM, VMEM],
        out_specs=[VMEM] * 4,
        scratch_shapes=[pltpu.VMEM((rows, width), BF), pltpu.SemaphoreType.DMA],
        compiler_params=pltpu.CompilerParams(vmem_limit_bytes=16 * 1024 * 1024),
        cost_estimate=SMALL,
        name="finish",
    )(base, over, gain.reshape(1, width))


UNIT_TILE = 256
COLUMN_TILE = 512
ROOM = pltpu.CompilerParams(vmem_limit_bytes=16 * 1024 * 1024)


def up_kernel(count, *refs):
    rows, (gate, upper, mine_out, theirs_out, stack, sems) = refs[:count], refs[count:]
    unit = mine_out.shape[0]
    copies, start = [], 0
    for at, ref in enumerate(rows):
        target = stack.at[pl.ds(start, ref.shape[0])]
        copies.append(pltpu.make_async_copy(ref, target, sems.at[at]))
        start += ref.shape[0]
    for copy in copies:
        copy.start()
    for copy in copies:
        copy.wait()

    def work(tile, carry):
        span = pl.ds(pl.multiple_of(tile * UNIT_TILE, UNIT_TILE), UNIT_TILE)
        both = dot(stack[...], jnp.concatenate([gate[:, span], upper[:, span]], axis=1))
        hidden = (jax.nn.silu(both[:, :UNIT_TILE]) * both[:, UNIT_TILE:]).astype(BF)
        mine_out[:, span] = hidden[:unit]
        theirs_out[:, span] = hidden[unit:]
        return carry

    lax.fori_loop(0, gate.shape[1] // UNIT_TILE, work, 0)


def mlp_up(mine, theirs, gate, upper):
    unit, width = sum(ref.shape[0] for ref in mine), gate.shape[0]
    count = len(mine) + len(theirs)
    return pl.pallas_call(
        functools.partial(up_kernel, count),
        out_shape=[jax.ShapeDtypeStruct((unit, gate.shape[1]), BF)] * 2,
        in_specs=[HBM] * count + [VMEM, VMEM],
        out_specs=[VMEM] * 2,
        scratch_shapes=[pltpu.VMEM((2 * unit, width), BF), pltpu.SemaphoreType.DMA((count,))],
        compiler_params=ROOM,
        cost_estimate=SMALL,
        name="mlp_up",
    )(*mine, *theirs, gate, upper)


def down_kernel(count, group, *refs):
    hidden, side, down = refs[:3]
    pieces, outs, stack = refs[3 : 3 + count], refs[3 + count : -1], refs[-1]
    units = hidden.shape[1]
    size = units // count
    stack[:, :units] = hidden[...]
    for at in range(count):
        start = pl.multiple_of((group[0] ^ at) * size, size)
        stack[:, units + at * size : units + (at + 1) * size] = side[:, pl.ds(start, size)]

    def work(tile, carry):
        span = pl.ds(pl.multiple_of(tile * COLUMN_TILE, COLUMN_TILE), COLUMN_TILE)
        weights = jnp.concatenate([down[:, span]] + [ref[:, span] for ref in pieces], axis=0)
        total = dot(stack[...], weights).astype(BF)
        at = 0
        for ref in outs:
            ref[:, span] = total[at : at + ref.shape[0]]
            at += ref.shape[0]
        return carry

    lax.fori_loop(0, down.shape[1] // COLUMN_TILE, work, 0)


def mlp_down(group, hidden, side, down, pieces, sizes):
    many, units = hidden.shape
    width = down.shape[1]
    return pl.pallas_call(
        functools.partial(down_kernel, len(pieces)),
        out_shape=[jax.ShapeDtypeStruct((size, width), BF) for size in sizes],
        in_specs=[SMEM] + [VMEM] * (3 + len(pieces)),
        out_specs=[VMEM] * len(sizes),
        scratch_shapes=[pltpu.VMEM((many, 2 * units), BF)],
        compiler_params=ROOM,
        cost_estimate=SMALL,
        name="mlp_down",
    )(group, hidden, side, down, *pieces)


def after(value, *others):
    return lax.optimization_barrier((value,) + others)[0]


def rows_of(w, index, count):
    size = w.shape[0] // count
    return lax.dynamic_slice_in_dim(w, index * size, size, 0)


def sync(*values):
    return lax.optimization_barrier(values)


def exchange_mlp(own, own_a, own_b, peers, groups, group, held, side_down):
    send = functools.partial(swap, axis="req", size=peers)
    cross = functools.partial(swap, axis="grp", size=groups, bit=1)
    over = functools.partial(swap, axis="grp", size=groups, bit=2)
    add = lambda *terms: sum(term.astype(F32) for term in terms)
    join = lambda *blocks: jnp.concatenate(blocks, axis=0)
    up = lambda mine, theirs: mlp_up(mine, theirs, held[0], held[1])
    unit = own.shape[0]
    half = unit // 2

    far_a = send(own_a, bit=4)
    near_a = send(own_a, bit=2)
    side = send(own, bit=1)
    side, near_a, far_a = sync(side, near_a, far_a)
    far_b = send(after(own_b, far_a), bit=4)
    both_a = send(far_a, bit=2)
    side_far_a = send(far_a, bit=1)
    side_near_a = send(near_a, bit=1)
    over_down = over(after(side_down, own))
    hidden_own, theirs_own = up([own], [side])
    side_far_a, side_near_a, far_b, both_a, _ = sync(
        side_far_a, side_near_a, far_b, both_a, hidden_own
    )
    both_b = send(far_b, bit=2)
    near_b = send(after(own_b, far_b), bit=2)
    side_far_b = send(far_b, bit=1)
    side_both_a = send(both_a, bit=1)
    hidden_a, theirs_a = up([far_a, near_a], [side_far_a, side_near_a])
    side_both_a, side_far_b, both_b, near_b, over_down, _ = sync(
        side_both_a, side_far_b, both_b, near_b, over_down, hidden_a
    )
    side_both_b = send(both_b, bit=1)
    pieces = [side_down, cross(side_down), over_down, cross(over_down)]
    down = lambda hidden, other, sizes: mlp_down(group, hidden, other, held[2], pieces, sizes)
    hidden_b, theirs_b = up([far_b, both_a], [side_far_b, side_both_a])
    from_b = send(theirs_b, bit=1)
    side_both_b, _ = sync(side_both_b, hidden_b)
    side_near_b = send(after(near_b, side_both_b), bit=1)
    hidden_c, theirs_c = up([both_b], [side_both_b])
    from_c = send(theirs_c, bit=1)
    from_b, _ = sync(from_b, hidden_c)
    sum_far_b, sum_both_a = down(hidden_b, from_b, [half, half])
    back_both_a = send(sum_both_a, bit=2)
    from_c, _ = sync(from_c, sum_both_a)
    from_a = send(after(theirs_a, from_c), bit=1)
    (sum_both_b,) = down(hidden_c, from_c, [half])
    back_both_b = send(sum_both_b, bit=2)
    side_near_b, _ = sync(side_near_b, sum_both_b)
    hidden_d, theirs_d = up([near_b], [side_near_b])
    from_d = send(theirs_d, bit=1)
    from_a, back_both_a, _ = sync(from_a, back_both_a, hidden_d)
    sum_far_a, sum_near_a = down(hidden_a, from_a, [half, half])
    total_a = add(sum_far_a, back_both_a).astype(BF)
    back_far_a = send(total_a, bit=4)
    back_near_a = send(sum_near_a, bit=2)
    back_both_b, _ = sync(back_both_b, total_a)
    total_b = add(sum_far_b, back_both_b).astype(BF)
    back_far_b = send(total_b, bit=4)
    from_own = send(after(theirs_own, total_b), bit=1)
    (sum_near_b,) = down(hidden_d, after(from_d, total_b), [half])
    back_near_b = send(sum_near_b, bit=2)
    (sum_own,) = down(hidden_own, after(from_own, sum_near_b), [unit])
    return add(
        sum_own, join(back_near_a, back_near_b), join(back_far_a, back_far_b)
    )


def body(
    hidden_in,
    attn_gain,
    mlp_gain,
    w_query,
    w_key,
    w_value,
    w_out,
    w_gate,
    w_up,
    w_down,
    cache_k,
    cache_v,
    owner_of_row,
    new_len,
    prior_len,
    page_table,
):
    peers = lax.axis_size("req")
    groups = lax.axis_size("grp")
    row_count = hidden_in.shape[0]
    pair = 2 * row_count // peers
    quarter = row_count // groups
    group_index = lax.axis_index("grp")
    owners = jnp.arange(peers, dtype=jnp.int32)

    member = owner_of_row[None, :] == owners[:, None]
    counts = jnp.sum(member.astype(jnp.int32), axis=1)
    row_ids = jnp.arange(row_count, dtype=jnp.int32)
    starts = jnp.min(jnp.where(member, row_ids[None, :], row_count), axis=1)
    cosines, sines = rope_tables(CONTEXT + pair)

    group = group_index.reshape(1)
    packed = pack_pages(page_table[0], prior_len[0], cache_k, cache_v)
    pages = lax.all_to_all(packed, "req", split_axis=0, concat_axis=0, tiled=True)
    query, fresh = project(starts, counts, after(hidden_in, cosines, sines), attn_gain, w_query, w_key, w_value, pair)
    if peers == 8:
        side_down = swap(rows_of(w_down, group_index, groups), "req", peers, 1)
    mixed = attend(
        starts, counts, group, query, fresh, pages, cosines, sines, row_count, groups
    )
    new = lax.all_to_all(after(fresh, pages), "req", split_axis=0, concat_axis=0, tiled=True)
    if peers == 8:
        mixed, side_down, new = sync(mixed, side_down, new)

    out_of = lambda part: dot(part, w_out).astype(BF)
    to_home = functools.partial(swap, axis="grp", size=groups)
    cross = out_of(mixed[3])
    later = after(mixed, cross)
    cross = to_home(cross, bit=1)
    over = (out_of(mixed[2]).astype(F32) + cross.astype(F32)).astype(BF)
    over = to_home(over, bit=2)
    beside = to_home(out_of(later[1]), bit=1)
    own_rows = lax.dynamic_slice_in_dim(hidden_in, group_index * quarter, quarter, 0).astype(F32)
    near_sum = out_of(later[0]).astype(F32) + beside.astype(F32)
    residual, own, own_a, own_b = finish(own_rows + RESIDUAL_MULT * near_sum, over, mlp_gain)
    if peers == 8:
        held = [w_gate, w_up, w_down]
        down = exchange_mlp(own, own_a, own_b, peers, groups, group, held, side_down)
    else:
        piece = lax.all_gather(own, "req", axis=0, tiled=True)
        part = feed_forward(piece, w_gate, w_up, w_down)
        down = lax.psum_scatter(part, "req", scatter_dimension=0, tiled=True).astype(F32)
    keys_out, values_out = store_new(page_table[0], prior_len[0], new_len[0], new, cosines, sines, cache_k, cache_v)
    layer_out = (residual + RESIDUAL_MULT * down).astype(BF)
    return (layer_out, keys_out, values_out)


def solution(mesh):
    in_specs = (
        P("req", None),
        P(),
        P(),
        P(None, "grp"),
        P(None, "grp"),
        P(None, "grp"),
        P("grp", None),
        P(None, "req"),
        P(None, "req"),
        P("req", None),
        P("req", None, "grp"),
        P("req", None, "grp"),
        P("req"),
        P("req", None),
        P("req", None),
        P("req", None),
    )
    out_specs = (P(("req", "grp"), None), P("req", None, "grp"), P("req", None, "grp"))
    return jax.shard_map(body, mesh=mesh, in_specs=in_specs, out_specs=out_specs, check_vma=False)
```

```python
import functools

import jax
import jax.numpy as jnp
from jax import lax
from jax.experimental import pallas as pl
from jax.experimental.pallas import tpu as pltpu
from jax.sharding import PartitionSpec as P

HD = 64
PAGE = 16
MAXP = 16
CONTEXT = 256
LANES = 128
INFO = 16


EPSILON = 1e-05
RESIDUAL_MULT = 0.22
SCORE_MULT = 0.015625
ROPE_BASE = 10000000.0
LOG2E = 1.4426950408889634
BF = jnp.bfloat16
F32 = jnp.float32
SMEM = pl.BlockSpec(memory_space=pltpu.SMEM)
VMEM = pl.BlockSpec(memory_space=pltpu.VMEM)
HBM = pl.BlockSpec(memory_space=pltpu.HBM)
SMALL = pl.CostEstimate(flops=0, bytes_accessed=0, transcendentals=0)


def normalize(values, gain):
    mean_square = jnp.mean(values * values, axis=-1, keepdims=True)
    return values * lax.rsqrt(mean_square + EPSILON) * gain


def rope_tables(length):
    lane = jnp.arange(LANES, dtype=jnp.int32)
    half = HD // 2
    freq = jnp.power(ROPE_BASE, -2.0 * (lane % half).astype(F32) / HD)
    angle = jnp.arange(length, dtype=jnp.int32).astype(F32)[:, None] * freq
    sign = jnp.where(lane % HD < half, -1.0, 1.0).astype(F32)
    return jnp.cos(angle), jnp.sin(angle) * sign


def rotate(values, cosine, sine):
    lane = lax.broadcasted_iota(jnp.int32, values.shape, 1)
    swapped = jnp.where(
        lane % HD < HD // 2,
        pltpu.roll(values, LANES - HD // 2, 1),
        pltpu.roll(values, HD // 2, 1),
    )
    return values * cosine + swapped * sine


def dot(a, b):
    return jnp.dot(a, b, preferred_element_type=F32)


def pack_kernel(table, prior, cache_k, cache_v, out):
    for source in range(out.shape[0]):
        for page in range(MAXP):
            at = table[source * MAXP + page]
            out[source, page * PAGE : (page + 1) * PAGE, :] = cache_k[at]
            out[source, CONTEXT + page * PAGE : CONTEXT + (page + 1) * PAGE, :] = cache_v[at]
        info = jnp.full((INFO, LANES), prior[source].astype(F32), F32)
        out[source, 2 * CONTEXT :, :] = info.astype(BF)


def pack_pages(table, prior, cache_k, cache_v):
    peers = prior.shape[0]
    return pl.pallas_call(
        pack_kernel,
        out_shape=jax.ShapeDtypeStruct((peers, 2 * CONTEXT + INFO, LANES), BF),
        in_specs=[SMEM, SMEM, VMEM, VMEM],
        out_specs=VMEM,
        compiler_params=pltpu.CompilerParams(vmem_limit_bytes=60 * 1024 * 1024),
        name="pack_pages",
        cost_estimate=SMALL,
    )(table, prior, cache_k, cache_v)


def one_hot(shape, start, count, slot_axis):
    slot = lax.broadcasted_iota(jnp.int32, shape, slot_axis)
    row = lax.broadcasted_iota(jnp.int32, shape, 1 - slot_axis)
    return jnp.where((row == slot + start) & (slot < count), 1.0, 0.0).astype(BF)


def project_kernel(starts, counts, hidden, gain, w_query, w_key, w_value, queries, news, whole):
    step = pl.program_id(0)
    rows = hidden.shape[0]
    qcols = w_query.shape[1]
    peers, pair, _ = queries.shape
    normed = normalize(hidden[...].astype(F32), gain[...]).astype(BF)
    here = pl.ds(pl.multiple_of(step * rows, rows), rows)
    whole[here, :qcols] = dot(normed, w_query[...]).astype(BF)
    whole[here, qcols : qcols + LANES] = dot(normed, w_key[...]).astype(BF)
    whole[here, qcols + LANES :] = dot(normed, w_value[...]).astype(BF)

    @pl.when(step == pl.num_programs(0) - 1)
    def _():
        def request(owner, carry):
            pick = one_hot((pair, whole.shape[0]), starts[owner], counts[owner], 0)
            slots = dot(pick, whole[...]).astype(BF)
            queries[owner] = slots[:, :qcols]
            news[owner] = slots[:, qcols:]
            return carry

        lax.fori_loop(0, peers, request, 0)


def project(starts, counts, hidden, gain, w_query, w_key, w_value, pair):
    rows, width = hidden.shape
    peers = starts.shape[0]
    qcols = w_query.shape[1]
    steps = 2
    whole = lambda step, *_: (0, 0)
    every = lambda step, *_: (0, 0, 0)
    return pl.pallas_call(
        project_kernel,
        out_shape=[
            jax.ShapeDtypeStruct((peers, pair, qcols), BF),
            jax.ShapeDtypeStruct((peers, pair, 2 * LANES), BF),
        ],
        grid_spec=pltpu.PrefetchScalarGridSpec(
            num_scalar_prefetch=2,
            grid=(steps,),
            in_specs=[
                pl.BlockSpec((rows // steps, width), lambda step, *_: (step, 0)),
                pl.BlockSpec((1, width), whole),
                pl.BlockSpec(w_query.shape, whole),
                pl.BlockSpec(w_key.shape, whole),
                pl.BlockSpec(w_value.shape, whole),
            ],
            out_specs=[
                pl.BlockSpec((peers, pair, qcols), every),
                pl.BlockSpec((peers, pair, 2 * LANES), every),
            ],
            scratch_shapes=[pltpu.VMEM((rows, qcols + 2 * LANES), BF)],
        ),
        compiler_params=pltpu.CompilerParams(
            vmem_limit_bytes=32 * 1024 * 1024, dimension_semantics=("arbitrary",)
        ),
        name="project",
        cost_estimate=SMALL,
    )(starts, counts, hidden, gain.reshape(1, width), w_query, w_key, w_value)


def attention_kernel(
    starts, counts, group, query, new, pages, cosines, sines, mixed, total, arrived, queries, news, sems
):
    step = pl.program_id(0)
    start, count = starts[step], counts[step]
    _, pair, qcols = query.shape
    rows = total.shape[1] - pair
    parts = mixed.shape[0]
    quarter = rows // parts

    def span(part):
        return pl.ds(pl.multiple_of((group[0] ^ part) * quarter, quarter), quarter)

    moved = ((query, queries), (new, news), (pages, arrived))

    @pl.when(step == 0)
    def _():
        for at in range(pages.shape[0]):
            for kind, (source, target) in enumerate(moved):
                pltpu.make_async_copy(source.at[at], target.at[at], sems.at[kind, at]).start()
        total[...] = jnp.zeros_like(total)

    for kind, (_, target) in enumerate(moved):
        pltpu.make_async_copy(target.at[step], target.at[step], sems.at[kind, step]).wait()

    def request(size):
        info = arrived[step, 2 * CONTEXT :, :].astype(F32)
        prior = jnp.max(info).astype(jnp.int32)
        cosine = cosines[pl.ds(prior, size), :]
        sine = sines[pl.ds(prior, size), :]
        new_key = rotate(news[step, :size, :LANES].astype(F32), cosine, sine).astype(BF)
        new_value = news[step, :size, LANES:]

        place = lax.broadcasted_iota(jnp.int32, (CONTEXT, size), 0)
        new_slot = lax.broadcasted_iota(jnp.int32, (CONTEXT, size), 1)
        put = jnp.where((place == new_slot + prior) & (new_slot < count), 1.0, 0.0).astype(BF)
        position = lax.broadcasted_iota(jnp.int32, (CONTEXT, LANES), 0)
        lane = lax.broadcasted_iota(jnp.int32, (CONTEXT, LANES), 1)
        low = lane < HD

        def merged(fresh, old):
            whole = jnp.where(position < prior, old.astype(F32), dot(put, fresh))
            turned = pltpu.roll(whole, HD, 1)
            return (
                jnp.where(low, whole, turned).astype(BF),
                jnp.where(low, turned, whole).astype(BF),
            )

        keys = merged(new_key, arrived[step, :CONTEXT, :])
        values = merged(new_value, arrived[step, CONTEXT : 2 * CONTEXT, :])

        query_slot = lax.broadcasted_iota(jnp.int32, (2 * size, CONTEXT), 0)
        query_slot = jnp.where(query_slot >= size, query_slot - size, query_slot)
        at = lax.broadcasted_iota(jnp.int32, (2 * size, CONTEXT), 1)
        allowed = at <= query_slot + prior
        left = lax.broadcasted_iota(jnp.int32, (size, LANES), 1) < HD
        slot = lax.broadcasted_iota(jnp.int32, (size, LANES), 0)
        tiles = qcols // LANES
        for tile in range(tiles):
            kv = tile * 2 // tiles
            span = slice(tile * LANES, (tile + 1) * LANES)
            turned = rotate(queries[step, :size, span].astype(F32), cosine, sine)
            both = jnp.concatenate([jnp.where(left, turned, 0.0), jnp.where(left, 0.0, turned)], 0)
            score = lax.dot_general(
                both.astype(BF), keys[kv], (((1,), (1,)), ((), ())), preferred_element_type=F32
            )
            score = jnp.where(allowed, score, -1e30)
            score = score - jnp.max(score, axis=-1, keepdims=True)
            weight = jnp.exp2(score * (SCORE_MULT * LOG2E))
            share = 1.0 / jnp.sum(weight, axis=-1, keepdims=True)
            probs = (weight * share).astype(BF)
            out = dot(probs, values[kv])
            out = jnp.where(left, out[:size], out[size:])
            rows_here = pl.ds(start, size)
            total[tile, rows_here] = jnp.where(slot < count, out, total[tile, rows_here])

    @pl.when(count > pair // 2)
    def _():
        request(pair)

    @pl.when((count > 0) & (count <= pair // 2))
    def _():
        request(pair // 2)

    @pl.when(step == pl.num_programs(0) - 1)
    def _():
        for part in range(parts):
            for tile in range(qcols // LANES):
                here = slice(tile * LANES, (tile + 1) * LANES)
                mixed[part, :, here] = total[tile, span(part), :].astype(BF)


def attend(starts, counts, group, query, new, pages, cosines, sines, rows, parts):
    peers, pair, qcols = query.shape
    whole = lambda step, *_: (0, 0)
    result = (parts, rows // parts, qcols)
    return pl.pallas_call(
        attention_kernel,
        out_shape=jax.ShapeDtypeStruct(result, BF),
        grid_spec=pltpu.PrefetchScalarGridSpec(
            num_scalar_prefetch=3,
            grid=(peers,),
            in_specs=[
                HBM,
                HBM,
                HBM,
                pl.BlockSpec(cosines.shape, whole),
                pl.BlockSpec(sines.shape, whole),
            ],
            out_specs=pl.BlockSpec(result, lambda step, *_: (0, 0, 0)),
            scratch_shapes=[
                pltpu.VMEM((qcols // LANES, rows + pair, LANES), F32),
                pltpu.VMEM(pages.shape, BF),
                pltpu.VMEM(query.shape, BF),
                pltpu.VMEM(new.shape, BF),
                pltpu.SemaphoreType.DMA((3, peers)),
            ],
        ),
        compiler_params=pltpu.CompilerParams(
            vmem_limit_bytes=60 * 1024 * 1024, dimension_semantics=("arbitrary",)
        ),
        name="attend",
        cost_estimate=SMALL,
    )(starts, counts, group, query, new, pages, cosines, sines)


def store_kernel(
    table, priors, counts, new, cosines, sines, cache_k, cache_v, keys_out, values_out
):
    peers, pair, _ = new.shape
    keys_out[...] = cache_k[...]
    values_out[...] = cache_v[...]

    def request(source, carry):
        prior, count = priors[source], counts[source]
        place = lax.broadcasted_iota(jnp.int32, (CONTEXT, pair), 0)
        slot = lax.broadcasted_iota(jnp.int32, (CONTEXT, pair), 1)
        put = jnp.where((place == slot + prior) & (slot < count), 1.0, 0.0).astype(BF)
        cosine = cosines[pl.ds(prior, pair), :]
        sine = sines[pl.ds(prior, pair), :]
        new_key = rotate(new[source, :, :LANES].astype(F32), cosine, sine).astype(BF)
        moved = dot(put, jnp.concatenate([new_key, new[source, :, LANES:]], axis=1))
        position = lax.broadcasted_iota(jnp.int32, (PAGE, LANES), 0)
        for page in range(MAXP):
            at = table[source * MAXP + page]
            here = position + page * PAGE
            fresh = (here >= prior) & (here < prior + count)
            rows = moved[page * PAGE : (page + 1) * PAGE]
            keys_out[at] = jnp.where(fresh, rows[:, :LANES], cache_k[at].astype(F32)).astype(BF)
            values_out[at] = jnp.where(fresh, rows[:, LANES:], cache_v[at].astype(F32)).astype(BF)
        return carry

    lax.fori_loop(0, peers, request, 0)


def store_new(table, priors, counts, new, cosines, sines, cache_k, cache_v):
    return pl.pallas_call(
        store_kernel,
        out_shape=[jax.ShapeDtypeStruct(cache_k.shape, BF)] * 2,
        in_specs=[SMEM] * 3 + [VMEM] * 5,
        out_specs=[VMEM] * 2,
        compiler_params=pltpu.CompilerParams(vmem_limit_bytes=32 * 1024 * 1024),
        name="store_new",
        cost_estimate=SMALL,
    )(table, priors, counts, new, cosines, sines, cache_k, cache_v)


def swap(values, axis, size, bit):
    return lax.ppermute(values, axis, [(at, at ^ bit) for at in range(size)])


def feed_forward(rows, w_gate, w_up, w_down):
    gate = dot(rows, w_gate)
    upper = dot(rows, w_up)
    hidden = (jax.nn.silu(gate) * upper).astype(BF)
    return dot(hidden, w_down).astype(BF)


def finish_kernel(base, over, gain, residual, own, own_a, own_b, arrived, sem):
    copy = pltpu.make_async_copy(over, arrived, sem)
    copy.start()
    copy.wait()
    half, block = own_a.shape[0], 16
    for at in range(0, own.shape[0], block):
        rows = slice(at, at + block)
        values = base[rows] + RESIDUAL_MULT * arrived[rows].astype(F32)
        residual[rows] = values
        normed = normalize(values, gain[...]).astype(BF)
        own[rows] = normed
        if at < half:
            own_a[rows] = normed
        else:
            own_b[at - half : at - half + block] = normed


def finish(base, over, gain):
    rows, width = base.shape
    shape = lambda count, kind: jax.ShapeDtypeStruct((count, width), kind)
    return pl.pallas_call(
        finish_kernel,
        out_shape=[shape(rows, F32), shape(rows, BF), shape(rows // 2, BF), shape(rows // 2, BF)],
        in_specs=[VMEM, HBM, VMEM],
        out_specs=[VMEM] * 4,
        scratch_shapes=[pltpu.VMEM((rows, width), BF), pltpu.SemaphoreType.DMA],
        compiler_params=pltpu.CompilerParams(vmem_limit_bytes=16 * 1024 * 1024),
        cost_estimate=SMALL,
        name="finish",
    )(base, over, gain.reshape(1, width))


UNIT_TILE = 256
COLUMN_TILE = 512
ROOM = pltpu.CompilerParams(vmem_limit_bytes=16 * 1024 * 1024)


def up_kernel(count, *refs):
    rows, (gate, upper, mine_out, theirs_out, stack, sems) = refs[:count], refs[count:]
    unit = mine_out.shape[0]
    copies, start = [], 0
    for at, ref in enumerate(rows):
        target = stack.at[pl.ds(start, ref.shape[0])]
        copies.append(pltpu.make_async_copy(ref, target, sems.at[at]))
        start += ref.shape[0]
    for copy in copies:
        copy.start()
    for copy in copies:
        copy.wait()

    def work(tile, carry):
        span = pl.ds(pl.multiple_of(tile * UNIT_TILE, UNIT_TILE), UNIT_TILE)
        both = dot(stack[...], jnp.concatenate([gate[:, span], upper[:, span]], axis=1))
        hidden = (jax.nn.silu(both[:, :UNIT_TILE]) * both[:, UNIT_TILE:]).astype(BF)
        mine_out[:, span] = hidden[:unit]
        theirs_out[:, span] = hidden[unit:]
        return carry

    lax.fori_loop(0, gate.shape[1] // UNIT_TILE, work, 0)


def mlp_up(mine, theirs, gate, upper):
    unit, width = sum(ref.shape[0] for ref in mine), gate.shape[0]
    count = len(mine) + len(theirs)
    return pl.pallas_call(
        functools.partial(up_kernel, count),
        out_shape=[jax.ShapeDtypeStruct((unit, gate.shape[1]), BF)] * 2,
        in_specs=[HBM] * count + [VMEM, VMEM],
        out_specs=[VMEM] * 2,
        scratch_shapes=[pltpu.VMEM((2 * unit, width), BF), pltpu.SemaphoreType.DMA((count,))],
        compiler_params=ROOM,
        cost_estimate=SMALL,
        name="mlp_up",
    )(*mine, *theirs, gate, upper)


def down_kernel(count, group, *refs):
    hidden, side, down = refs[:3]
    pieces, outs, stack = refs[3 : 3 + count], refs[3 + count : -1], refs[-1]
    units = hidden.shape[1]
    size = units // count
    stack[:, :units] = hidden[...]
    for at in range(count):
        start = pl.multiple_of((group[0] ^ at) * size, size)
        stack[:, units + at * size : units + (at + 1) * size] = side[:, pl.ds(start, size)]

    def work(tile, carry):
        span = pl.ds(pl.multiple_of(tile * COLUMN_TILE, COLUMN_TILE), COLUMN_TILE)
        weights = jnp.concatenate([down[:, span]] + [ref[:, span] for ref in pieces], axis=0)
        total = dot(stack[...], weights).astype(BF)
        at = 0
        for ref in outs:
            ref[:, span] = total[at : at + ref.shape[0]]
            at += ref.shape[0]
        return carry

    lax.fori_loop(0, down.shape[1] // COLUMN_TILE, work, 0)


def mlp_down(group, hidden, side, down, pieces, sizes):
    many, units = hidden.shape
    width = down.shape[1]
    return pl.pallas_call(
        functools.partial(down_kernel, len(pieces)),
        out_shape=[jax.ShapeDtypeStruct((size, width), BF) for size in sizes],
        in_specs=[SMEM] + [VMEM] * (3 + len(pieces)),
        out_specs=[VMEM] * len(sizes),
        scratch_shapes=[pltpu.VMEM((many, 2 * units), BF)],
        compiler_params=ROOM,
        cost_estimate=SMALL,
        name="mlp_down",
    )(group, hidden, side, down, *pieces)


def after(value, *others):
    return lax.optimization_barrier((value,) + others)[0]


def rows_of(w, index, count):
    size = w.shape[0] // count
    return lax.dynamic_slice_in_dim(w, index * size, size, 0)


def sync(*values):
    return lax.optimization_barrier(values)


def exchange_mlp(own, own_a, own_b, peers, groups, group, held, side_down):
    send = functools.partial(swap, axis="req", size=peers)
    cross = functools.partial(swap, axis="grp", size=groups, bit=1)
    over = functools.partial(swap, axis="grp", size=groups, bit=2)
    add = lambda *terms: sum(term.astype(F32) for term in terms)
    join = lambda *blocks: jnp.concatenate(blocks, axis=0)
    up = lambda mine, theirs: mlp_up(mine, theirs, held[0], held[1])
    unit = own.shape[0]
    half = unit // 2

    far_a = send(own_a, bit=4)
    near_a = send(own_a, bit=2)
    side = send(own, bit=1)
    side, near_a, far_a = sync(side, near_a, far_a)
    far_b = send(after(own_b, far_a), bit=4)
    both_a = send(far_a, bit=2)
    side_far_a = send(far_a, bit=1)
    side_near_a = send(near_a, bit=1)
    over_down = over(after(side_down, own))
    hidden_own, theirs_own = up([own], [side])
    side_far_a, side_near_a, far_b, both_a, _ = sync(
        side_far_a, side_near_a, far_b, both_a, hidden_own
    )
    both_b = send(far_b, bit=2)
    near_b = send(after(own_b, far_b), bit=2)
    side_far_b = send(far_b, bit=1)
    side_both_a = send(both_a, bit=1)
    hidden_a, theirs_a = up([far_a, near_a], [side_far_a, side_near_a])
    side_both_a, side_far_b, both_b, near_b, over_down, _ = sync(
        side_both_a, side_far_b, both_b, near_b, over_down, hidden_a
    )
    side_both_b = send(both_b, bit=1)
    pieces = [side_down, cross(side_down), over_down, cross(over_down)]
    down = lambda hidden, other, sizes: mlp_down(group, hidden, other, held[2], pieces, sizes)
    hidden_b, theirs_b = up([far_b, both_a], [side_far_b, side_both_a])
    from_b = send(theirs_b, bit=1)
    side_both_b, _ = sync(side_both_b, hidden_b)
    from_a = send(after(theirs_a, side_both_b), bit=1)
    hidden_c, theirs_c = up([both_b], [side_both_b])
    from_c = send(theirs_c, bit=1)
    from_b, _ = sync(from_b, hidden_c)
    sum_far_b, sum_both_a = down(hidden_b, from_b, [half, half])
    back_both_a = send(sum_both_a, bit=2)
    from_c, _ = sync(from_c, sum_both_a)
    side_near_b = send(after(near_b, from_c), bit=1)
    (sum_both_b,) = down(hidden_c, from_c, [half])
    back_both_b = send(sum_both_b, bit=2)
    from_a, _ = sync(from_a, sum_both_b)
    sum_far_a, sum_near_a = down(hidden_a, from_a, [half, half])
    back_near_a = send(sum_near_a, bit=2)
    side_near_b, _ = sync(side_near_b, sum_near_a)
    hidden_d, theirs_d = up([near_b], [side_near_b])
    from_d = send(theirs_d, bit=1)
    back_both_a, _ = sync(back_both_a, hidden_d)
    total_a = add(sum_far_a, back_both_a).astype(BF)
    back_far_a = send(total_a, bit=4)
    back_both_b, _ = sync(back_both_b, total_a)
    total_b = add(sum_far_b, back_both_b).astype(BF)
    back_far_b = send(total_b, bit=4)
    from_own = send(after(theirs_own, total_b), bit=1)
    (sum_near_b,) = down(hidden_d, after(from_d, total_b), [half])
    back_near_b = send(sum_near_b, bit=2)
    (sum_own,) = down(hidden_own, after(from_own, sum_near_b), [unit])
    return add(
        sum_own, join(back_near_a, back_near_b), join(back_far_a, back_far_b)
    )


def body(
    hidden_in,
    attn_gain,
    mlp_gain,
    w_query,
    w_key,
    w_value,
    w_out,
    w_gate,
    w_up,
    w_down,
    cache_k,
    cache_v,
    owner_of_row,
    new_len,
    prior_len,
    page_table,
):
    peers = lax.axis_size("req")
    groups = lax.axis_size("grp")
    row_count = hidden_in.shape[0]
    pair = 2 * row_count // peers
    quarter = row_count // groups
    group_index = lax.axis_index("grp")
    owners = jnp.arange(peers, dtype=jnp.int32)

    member = owner_of_row[None, :] == owners[:, None]
    counts = jnp.sum(member.astype(jnp.int32), axis=1)
    row_ids = jnp.arange(row_count, dtype=jnp.int32)
    starts = jnp.min(jnp.where(member, row_ids[None, :], row_count), axis=1)
    cosines, sines = rope_tables(CONTEXT + pair)

    group = group_index.reshape(1)
    packed = pack_pages(page_table[0], prior_len[0], cache_k, cache_v)
    pages = lax.all_to_all(packed, "req", split_axis=0, concat_axis=0, tiled=True)
    query, fresh = project(starts, counts, after(hidden_in, cosines, sines), attn_gain, w_query, w_key, w_value, pair)
    if peers == 8:
        side_down = swap(rows_of(w_down, group_index, groups), "req", peers, 1)
    mixed = attend(
        starts, counts, group, query, fresh, pages, cosines, sines, row_count, groups
    )
    new = lax.all_to_all(after(fresh, pages), "req", split_axis=0, concat_axis=0, tiled=True)
    if peers == 8:
        mixed, side_down, new = sync(mixed, side_down, new)

    out_of = lambda part: dot(part, w_out).astype(BF)
    to_home = functools.partial(swap, axis="grp", size=groups)
    cross = out_of(mixed[3])
    later = after(mixed, cross)
    cross = to_home(cross, bit=1)
    over = (out_of(later[2]).astype(F32) + cross.astype(F32)).astype(BF)
    over = to_home(over, bit=2)
    beside = to_home(out_of(later[1]), bit=1)
    own_rows = lax.dynamic_slice_in_dim(hidden_in, group_index * quarter, quarter, 0).astype(F32)
    near_sum = out_of(later[0]).astype(F32) + beside.astype(F32)
    residual, own, own_a, own_b = finish(own_rows + RESIDUAL_MULT * near_sum, over, mlp_gain)
    if peers == 8:
        held = [w_gate, w_up, w_down]
        down = exchange_mlp(own, own_a, own_b, peers, groups, group, held, side_down)
    else:
        piece = lax.all_gather(own, "req", axis=0, tiled=True)
        part = feed_forward(piece, w_gate, w_up, w_down)
        down = lax.psum_scatter(part, "req", scatter_dimension=0, tiled=True).astype(F32)
    keys_out, values_out = store_new(page_table[0], prior_len[0], new_len[0], new, cosines, sines, cache_k, cache_v)
    layer_out = (residual + RESIDUAL_MULT * down).astype(BF)
    return (layer_out, keys_out, values_out)


def solution(mesh):
    in_specs = (
        P("req", None),
        P(),
        P(),
        P(None, "grp"),
        P(None, "grp"),
        P(None, "grp"),
        P("grp", None),
        P(None, "req"),
        P(None, "req"),
        P("req", None),
        P("req", None, "grp"),
        P("req", None, "grp"),
        P("req"),
        P("req", None),
        P("req", None),
        P("req", None),
    )
    out_specs = (P(("req", "grp"), None), P("req", None, "grp"), P("req", None, "grp"))
    return jax.shard_map(body, mesh=mesh, in_specs=in_specs, out_specs=out_specs, check_vma=False)
```

```python
import functools

import jax
import jax.numpy as jnp
from jax import lax
from jax.experimental import pallas as pl
from jax.experimental.pallas import tpu as pltpu
from jax.sharding import PartitionSpec as P

HD = 64
PAGE = 16
MAXP = 16
CONTEXT = 256
LANES = 128
INFO = 16


EPSILON = 1e-05
RESIDUAL_MULT = 0.22
SCORE_MULT = 0.015625
ROPE_BASE = 10000000.0
LOG2E = 1.4426950408889634
BF = jnp.bfloat16
F32 = jnp.float32
SMEM = pl.BlockSpec(memory_space=pltpu.SMEM)
VMEM = pl.BlockSpec(memory_space=pltpu.VMEM)
HBM = pl.BlockSpec(memory_space=pltpu.HBM)
SMALL = pl.CostEstimate(flops=0, bytes_accessed=0, transcendentals=0)


def normalize(values, gain):
    mean_square = jnp.mean(values * values, axis=-1, keepdims=True)
    return values * lax.rsqrt(mean_square + EPSILON) * gain


def rope_tables(length):
    lane = jnp.arange(LANES, dtype=jnp.int32)
    half = HD // 2
    freq = jnp.power(ROPE_BASE, -2.0 * (lane % half).astype(F32) / HD)
    angle = jnp.arange(length, dtype=jnp.int32).astype(F32)[:, None] * freq
    sign = jnp.where(lane % HD < half, -1.0, 1.0).astype(F32)
    return jnp.cos(angle), jnp.sin(angle) * sign


def rotate(values, cosine, sine):
    lane = lax.broadcasted_iota(jnp.int32, values.shape, 1)
    swapped = jnp.where(
        lane % HD < HD // 2,
        pltpu.roll(values, LANES - HD // 2, 1),
        pltpu.roll(values, HD // 2, 1),
    )
    return values * cosine + swapped * sine


def dot(a, b):
    return jnp.dot(a, b, preferred_element_type=F32)


def pack_kernel(table, prior, cache_k, cache_v, out):
    for source in range(out.shape[0]):
        for page in range(MAXP):
            at = table[source * MAXP + page]
            out[source, page * PAGE : (page + 1) * PAGE, :] = cache_k[at]
            out[source, CONTEXT + page * PAGE : CONTEXT + (page + 1) * PAGE, :] = cache_v[at]
        info = jnp.full((INFO, LANES), prior[source].astype(F32), F32)
        out[source, 2 * CONTEXT :, :] = info.astype(BF)


def pack_pages(table, prior, cache_k, cache_v):
    peers = prior.shape[0]
    return pl.pallas_call(
        pack_kernel,
        out_shape=jax.ShapeDtypeStruct((peers, 2 * CONTEXT + INFO, LANES), BF),
        in_specs=[SMEM, SMEM, VMEM, VMEM],
        out_specs=VMEM,
        compiler_params=pltpu.CompilerParams(vmem_limit_bytes=60 * 1024 * 1024),
        name="pack_pages",
        cost_estimate=SMALL,
    )(table, prior, cache_k, cache_v)


def one_hot(shape, start, count, slot_axis):
    slot = lax.broadcasted_iota(jnp.int32, shape, slot_axis)
    row = lax.broadcasted_iota(jnp.int32, shape, 1 - slot_axis)
    return jnp.where((row == slot + start) & (slot < count), 1.0, 0.0).astype(BF)


def project_kernel(starts, counts, hidden, gain, w_query, w_key, w_value, queries, news, whole):
    step = pl.program_id(0)
    rows = hidden.shape[0]
    qcols = w_query.shape[1]
    peers, pair, _ = queries.shape
    normed = normalize(hidden[...].astype(F32), gain[...]).astype(BF)
    here = pl.ds(pl.multiple_of(step * rows, rows), rows)
    whole[here, :qcols] = dot(normed, w_query[...]).astype(BF)
    whole[here, qcols : qcols + LANES] = dot(normed, w_key[...]).astype(BF)
    whole[here, qcols + LANES :] = dot(normed, w_value[...]).astype(BF)

    @pl.when(step == pl.num_programs(0) - 1)
    def _():
        def request(owner, carry):
            pick = one_hot((pair, whole.shape[0]), starts[owner], counts[owner], 0)
            slots = dot(pick, whole[...]).astype(BF)
            queries[owner] = slots[:, :qcols]
            news[owner] = slots[:, qcols:]
            return carry

        lax.fori_loop(0, peers, request, 0)


def project(starts, counts, hidden, gain, w_query, w_key, w_value, pair):
    rows, width = hidden.shape
    peers = starts.shape[0]
    qcols = w_query.shape[1]
    steps = 2
    whole = lambda step, *_: (0, 0)
    every = lambda step, *_: (0, 0, 0)
    return pl.pallas_call(
        project_kernel,
        out_shape=[
            jax.ShapeDtypeStruct((peers, pair, qcols), BF),
            jax.ShapeDtypeStruct((peers, pair, 2 * LANES), BF),
        ],
        grid_spec=pltpu.PrefetchScalarGridSpec(
            num_scalar_prefetch=2,
            grid=(steps,),
            in_specs=[
                pl.BlockSpec((rows // steps, width), lambda step, *_: (step, 0)),
                pl.BlockSpec((1, width), whole),
                pl.BlockSpec(w_query.shape, whole),
                pl.BlockSpec(w_key.shape, whole),
                pl.BlockSpec(w_value.shape, whole),
            ],
            out_specs=[
                pl.BlockSpec((peers, pair, qcols), every),
                pl.BlockSpec((peers, pair, 2 * LANES), every),
            ],
            scratch_shapes=[pltpu.VMEM((rows, qcols + 2 * LANES), BF)],
        ),
        compiler_params=pltpu.CompilerParams(
            vmem_limit_bytes=32 * 1024 * 1024, dimension_semantics=("arbitrary",)
        ),
        name="project",
        cost_estimate=SMALL,
    )(starts, counts, hidden, gain.reshape(1, width), w_query, w_key, w_value)


def attention_kernel(
    starts, counts, group, query, new, pages, cosines, sines, mixed, total, arrived, queries, news, sems
):
    step = pl.program_id(0)
    start, count = starts[step], counts[step]
    _, pair, qcols = query.shape
    rows = total.shape[1] - pair
    parts = mixed.shape[0]
    quarter = rows // parts

    def span(part):
        return pl.ds(pl.multiple_of((group[0] ^ part) * quarter, quarter), quarter)

    moved = ((query, queries), (new, news), (pages, arrived))

    @pl.when(step == 0)
    def _():
        for at in range(pages.shape[0]):
            for kind, (source, target) in enumerate(moved):
                pltpu.make_async_copy(source.at[at], target.at[at], sems.at[kind, at]).start()
        total[...] = jnp.zeros_like(total)

    for kind, (_, target) in enumerate(moved):
        pltpu.make_async_copy(target.at[step], target.at[step], sems.at[kind, step]).wait()

    def request(size):
        info = arrived[step, 2 * CONTEXT :, :].astype(F32)
        prior = jnp.max(info).astype(jnp.int32)
        cosine = cosines[pl.ds(prior, size), :]
        sine = sines[pl.ds(prior, size), :]
        new_key = rotate(news[step, :size, :LANES].astype(F32), cosine, sine).astype(BF)
        new_value = news[step, :size, LANES:]

        place = lax.broadcasted_iota(jnp.int32, (CONTEXT, size), 0)
        new_slot = lax.broadcasted_iota(jnp.int32, (CONTEXT, size), 1)
        put = jnp.where((place == new_slot + prior) & (new_slot < count), 1.0, 0.0).astype(BF)
        position = lax.broadcasted_iota(jnp.int32, (CONTEXT, LANES), 0)
        lane = lax.broadcasted_iota(jnp.int32, (CONTEXT, LANES), 1)
        low = lane < HD

        def merged(fresh, old):
            whole = jnp.where(position < prior, old.astype(F32), dot(put, fresh))
            turned = pltpu.roll(whole, HD, 1)
            return (
                jnp.where(low, whole, turned).astype(BF),
                jnp.where(low, turned, whole).astype(BF),
            )

        keys = merged(new_key, arrived[step, :CONTEXT, :])
        values = merged(new_value, arrived[step, CONTEXT : 2 * CONTEXT, :])

        query_slot = lax.broadcasted_iota(jnp.int32, (2 * size, CONTEXT), 0)
        query_slot = jnp.where(query_slot >= size, query_slot - size, query_slot)
        at = lax.broadcasted_iota(jnp.int32, (2 * size, CONTEXT), 1)
        allowed = at <= query_slot + prior
        left = lax.broadcasted_iota(jnp.int32, (size, LANES), 1) < HD
        slot = lax.broadcasted_iota(jnp.int32, (size, LANES), 0)
        tiles = qcols // LANES
        for tile in range(tiles):
            kv = tile * 2 // tiles
            span = slice(tile * LANES, (tile + 1) * LANES)
            turned = rotate(queries[step, :size, span].astype(F32), cosine, sine)
            both = jnp.concatenate([jnp.where(left, turned, 0.0), jnp.where(left, 0.0, turned)], 0)
            score = lax.dot_general(
                both.astype(BF), keys[kv], (((1,), (1,)), ((), ())), preferred_element_type=F32
            )
            score = jnp.where(allowed, score, -1e30)
            score = score - jnp.max(score, axis=-1, keepdims=True)
            weight = jnp.exp2(score * (SCORE_MULT * LOG2E))
            share = 1.0 / jnp.sum(weight, axis=-1, keepdims=True)
            probs = (weight * share).astype(BF)
            out = dot(probs, values[kv])
            out = jnp.where(left, out[:size], out[size:])
            rows_here = pl.ds(start, size)
            total[tile, rows_here] = jnp.where(slot < count, out, total[tile, rows_here])

    @pl.when(count > pair // 2)
    def _():
        request(pair)

    @pl.when((count > 0) & (count <= pair // 2))
    def _():
        request(pair // 2)

    @pl.when(step == pl.num_programs(0) - 1)
    def _():
        for part in range(parts):
            for tile in range(qcols // LANES):
                here = slice(tile * LANES, (tile + 1) * LANES)
                mixed[part, :, here] = total[tile, span(part), :].astype(BF)


def attend(starts, counts, group, query, new, pages, cosines, sines, rows, parts):
    peers, pair, qcols = query.shape
    whole = lambda step, *_: (0, 0)
    result = (parts, rows // parts, qcols)
    return pl.pallas_call(
        attention_kernel,
        out_shape=jax.ShapeDtypeStruct(result, BF),
        grid_spec=pltpu.PrefetchScalarGridSpec(
            num_scalar_prefetch=3,
            grid=(peers,),
            in_specs=[
                HBM,
                HBM,
                HBM,
                pl.BlockSpec(cosines.shape, whole),
                pl.BlockSpec(sines.shape, whole),
            ],
            out_specs=pl.BlockSpec(result, lambda step, *_: (0, 0, 0)),
            scratch_shapes=[
                pltpu.VMEM((qcols // LANES, rows + pair, LANES), F32),
                pltpu.VMEM(pages.shape, BF),
                pltpu.VMEM(query.shape, BF),
                pltpu.VMEM(new.shape, BF),
                pltpu.SemaphoreType.DMA((3, peers)),
            ],
        ),
        compiler_params=pltpu.CompilerParams(
            vmem_limit_bytes=60 * 1024 * 1024, dimension_semantics=("arbitrary",)
        ),
        name="attend",
        cost_estimate=SMALL,
    )(starts, counts, group, query, new, pages, cosines, sines)


def store_kernel(
    table, priors, counts, new, cosines, sines, cache_k, cache_v, keys_out, values_out
):
    peers, pair, _ = new.shape
    keys_out[...] = cache_k[...]
    values_out[...] = cache_v[...]

    def request(source, carry):
        prior, count = priors[source], counts[source]
        place = lax.broadcasted_iota(jnp.int32, (CONTEXT, pair), 0)
        slot = lax.broadcasted_iota(jnp.int32, (CONTEXT, pair), 1)
        put = jnp.where((place == slot + prior) & (slot < count), 1.0, 0.0).astype(BF)
        cosine = cosines[pl.ds(prior, pair), :]
        sine = sines[pl.ds(prior, pair), :]
        new_key = rotate(new[source, :, :LANES].astype(F32), cosine, sine).astype(BF)
        moved = dot(put, jnp.concatenate([new_key, new[source, :, LANES:]], axis=1))
        position = lax.broadcasted_iota(jnp.int32, (PAGE, LANES), 0)
        for page in range(MAXP):
            at = table[source * MAXP + page]
            here = position + page * PAGE
            fresh = (here >= prior) & (here < prior + count)
            rows = moved[page * PAGE : (page + 1) * PAGE]
            keys_out[at] = jnp.where(fresh, rows[:, :LANES], cache_k[at].astype(F32)).astype(BF)
            values_out[at] = jnp.where(fresh, rows[:, LANES:], cache_v[at].astype(F32)).astype(BF)
        return carry

    lax.fori_loop(0, peers, request, 0)


def store_new(table, priors, counts, new, cosines, sines, cache_k, cache_v):
    return pl.pallas_call(
        store_kernel,
        out_shape=[jax.ShapeDtypeStruct(cache_k.shape, BF)] * 2,
        in_specs=[SMEM] * 3 + [VMEM] * 5,
        out_specs=[VMEM] * 2,
        compiler_params=pltpu.CompilerParams(vmem_limit_bytes=32 * 1024 * 1024),
        name="store_new",
        cost_estimate=SMALL,
    )(table, priors, counts, new, cosines, sines, cache_k, cache_v)


def swap(values, axis, size, bit):
    return lax.ppermute(values, axis, [(at, at ^ bit) for at in range(size)])


def feed_forward(rows, w_gate, w_up, w_down):
    gate = dot(rows, w_gate)
    upper = dot(rows, w_up)
    hidden = (jax.nn.silu(gate) * upper).astype(BF)
    return dot(hidden, w_down).astype(BF)


def finish_kernel(base, over, gain, residual, own, own_a, own_b, arrived, sem):
    copy = pltpu.make_async_copy(over, arrived, sem)
    copy.start()
    copy.wait()
    half, block = own_a.shape[0], 16
    for at in range(0, own.shape[0], block):
        rows = slice(at, at + block)
        values = base[rows] + RESIDUAL_MULT * arrived[rows].astype(F32)
        residual[rows] = values
        normed = normalize(values, gain[...]).astype(BF)
        own[rows] = normed
        if at < half:
            own_a[rows] = normed
        else:
            own_b[at - half : at - half + block] = normed


def finish(base, over, gain):
    rows, width = base.shape
    shape = lambda count, kind: jax.ShapeDtypeStruct((count, width), kind)
    return pl.pallas_call(
        finish_kernel,
        out_shape=[shape(rows, F32), shape(rows, BF), shape(rows // 2, BF), shape(rows // 2, BF)],
        in_specs=[VMEM, HBM, VMEM],
        out_specs=[VMEM] * 4,
        scratch_shapes=[pltpu.VMEM((rows, width), BF), pltpu.SemaphoreType.DMA],
        compiler_params=pltpu.CompilerParams(vmem_limit_bytes=16 * 1024 * 1024),
        cost_estimate=SMALL,
        name="finish",
    )(base, over, gain.reshape(1, width))


UNIT_TILE = 256
COLUMN_TILE = 512
ROOM = pltpu.CompilerParams(vmem_limit_bytes=16 * 1024 * 1024)


def up_kernel(count, *refs):
    rows, (gate, upper, mine_out, theirs_out, stack, sems) = refs[:count], refs[count:]
    unit = mine_out.shape[0]
    copies, start = [], 0
    for at, ref in enumerate(rows):
        target = stack.at[pl.ds(start, ref.shape[0])]
        copies.append(pltpu.make_async_copy(ref, target, sems.at[at]))
        start += ref.shape[0]
    for copy in copies:
        copy.start()
    for copy in copies:
        copy.wait()

    def work(tile, carry):
        span = pl.ds(pl.multiple_of(tile * UNIT_TILE, UNIT_TILE), UNIT_TILE)
        both = dot(stack[...], jnp.concatenate([gate[:, span], upper[:, span]], axis=1))
        hidden = (jax.nn.silu(both[:, :UNIT_TILE]) * both[:, UNIT_TILE:]).astype(BF)
        mine_out[:, span] = hidden[:unit]
        theirs_out[:, span] = hidden[unit:]
        return carry

    lax.fori_loop(0, gate.shape[1] // UNIT_TILE, work, 0)


def mlp_up(mine, theirs, gate, upper):
    unit, width = sum(ref.shape[0] for ref in mine), gate.shape[0]
    count = len(mine) + len(theirs)
    return pl.pallas_call(
        functools.partial(up_kernel, count),
        out_shape=[jax.ShapeDtypeStruct((unit, gate.shape[1]), BF)] * 2,
        in_specs=[HBM] * count + [VMEM, VMEM],
        out_specs=[VMEM] * 2,
        scratch_shapes=[pltpu.VMEM((2 * unit, width), BF), pltpu.SemaphoreType.DMA((count,))],
        compiler_params=ROOM,
        cost_estimate=SMALL,
        name="mlp_up",
    )(*mine, *theirs, gate, upper)


def down_kernel(count, group, *refs):
    hidden, side, down = refs[:3]
    pieces, outs, stack = refs[3 : 3 + count], refs[3 + count : -1], refs[-1]
    units = hidden.shape[1]
    size = units // count
    stack[:, :units] = hidden[...]
    for at in range(count):
        start = pl.multiple_of((group[0] ^ at) * size, size)
        stack[:, units + at * size : units + (at + 1) * size] = side[:, pl.ds(start, size)]

    def work(tile, carry):
        span = pl.ds(pl.multiple_of(tile * COLUMN_TILE, COLUMN_TILE), COLUMN_TILE)
        weights = jnp.concatenate([down[:, span]] + [ref[:, span] for ref in pieces], axis=0)
        total = dot(stack[...], weights).astype(BF)
        at = 0
        for ref in outs:
            ref[:, span] = total[at : at + ref.shape[0]]
            at += ref.shape[0]
        return carry

    lax.fori_loop(0, down.shape[1] // COLUMN_TILE, work, 0)


def mlp_down(group, hidden, side, down, pieces, sizes):
    many, units = hidden.shape
    width = down.shape[1]
    return pl.pallas_call(
        functools.partial(down_kernel, len(pieces)),
        out_shape=[jax.ShapeDtypeStruct((size, width), BF) for size in sizes],
        in_specs=[SMEM] + [VMEM] * (3 + len(pieces)),
        out_specs=[VMEM] * len(sizes),
        scratch_shapes=[pltpu.VMEM((many, 2 * units), BF)],
        compiler_params=ROOM,
        cost_estimate=SMALL,
        name="mlp_down",
    )(group, hidden, side, down, *pieces)


def after(value, *others):
    return lax.optimization_barrier((value,) + others)[0]


def rows_of(w, index, count):
    size = w.shape[0] // count
    return lax.dynamic_slice_in_dim(w, index * size, size, 0)


def sync(*values):
    return lax.optimization_barrier(values)


def exchange_mlp(own, own_a, own_b, peers, groups, group, held, side_down):
    send = functools.partial(swap, axis="req", size=peers)
    cross = functools.partial(swap, axis="grp", size=groups, bit=1)
    over = functools.partial(swap, axis="grp", size=groups, bit=2)
    add = lambda *terms: sum(term.astype(F32) for term in terms)
    join = lambda *blocks: jnp.concatenate(blocks, axis=0)
    up = lambda mine, theirs: mlp_up(mine, theirs, held[0], held[1])
    unit = own.shape[0]
    half = unit // 2

    far_a = send(own_a, bit=4)
    near_a = send(own_a, bit=2)
    side = send(own, bit=1)
    side, near_a, far_a = sync(side, near_a, far_a)
    far_b = send(after(own_b, far_a), bit=4)
    both_a = send(far_a, bit=2)
    side_far_a = send(far_a, bit=1)
    side_near_a = send(near_a, bit=1)
    over_down = over(after(side_down, far_a))
    hidden_own, theirs_own = up([own], [side])
    side_far_a, side_near_a, far_b, both_a, _ = sync(
        side_far_a, side_near_a, far_b, both_a, hidden_own
    )
    both_b = send(far_b, bit=2)
    near_b = send(after(own_b, far_b), bit=2)
    side_far_b = send(far_b, bit=1)
    side_both_a = send(both_a, bit=1)
    hidden_a, theirs_a = up([far_a, near_a], [side_far_a, side_near_a])
    side_both_a, side_far_b, both_b, near_b, over_down, _ = sync(
        side_both_a, side_far_b, both_b, near_b, over_down, hidden_a
    )
    side_both_b = send(both_b, bit=1)
    pieces = [side_down, cross(side_down), over_down, cross(over_down)]
    down = lambda hidden, other, sizes: mlp_down(group, hidden, other, held[2], pieces, sizes)
    hidden_b, theirs_b = up([far_b, both_a], [side_far_b, side_both_a])
    from_b = send(theirs_b, bit=1)
    side_both_b, _ = sync(side_both_b, hidden_b)
    from_a = send(after(theirs_a, side_both_b), bit=1)
    hidden_c, theirs_c = up([both_b], [side_both_b])
    from_c = send(theirs_c, bit=1)
    from_b, _ = sync(from_b, hidden_c)
    sum_far_b, sum_both_a = down(hidden_b, from_b, [half, half])
    back_both_a = send(sum_both_a, bit=2)
    from_c, _ = sync(from_c, sum_both_a)
    side_near_b = send(after(near_b, from_c), bit=1)
    (sum_both_b,) = down(hidden_c, from_c, [half])
    back_both_b = send(sum_both_b, bit=2)
    from_a, _ = sync(from_a, sum_both_b)
    sum_far_a, sum_near_a = down(hidden_a, from_a, [half, half])
    back_near_a = send(sum_near_a, bit=2)
    side_near_b, _ = sync(side_near_b, sum_near_a)
    hidden_d, theirs_d = up([near_b], [side_near_b])
    from_d = send(theirs_d, bit=1)
    back_both_a, _ = sync(back_both_a, hidden_d)
    total_a = add(sum_far_a, back_both_a).astype(BF)
    back_far_a = send(total_a, bit=4)
    back_both_b, _ = sync(back_both_b, total_a)
    total_b = add(sum_far_b, back_both_b).astype(BF)
    back_far_b = send(total_b, bit=4)
    from_own = send(after(theirs_own, total_b), bit=1)
    (sum_near_b,) = down(hidden_d, after(from_d, total_b), [half])
    back_near_b = send(sum_near_b, bit=2)
    (sum_own,) = down(hidden_own, after(from_own, sum_near_b), [unit])
    return add(
        sum_own, join(back_near_a, back_near_b), join(back_far_a, back_far_b)
    )


def body(
    hidden_in,
    attn_gain,
    mlp_gain,
    w_query,
    w_key,
    w_value,
    w_out,
    w_gate,
    w_up,
    w_down,
    cache_k,
    cache_v,
    owner_of_row,
    new_len,
    prior_len,
    page_table,
):
    peers = lax.axis_size("req")
    groups = lax.axis_size("grp")
    row_count = hidden_in.shape[0]
    pair = 2 * row_count // peers
    quarter = row_count // groups
    group_index = lax.axis_index("grp")
    owners = jnp.arange(peers, dtype=jnp.int32)

    member = owner_of_row[None, :] == owners[:, None]
    counts = jnp.sum(member.astype(jnp.int32), axis=1)
    row_ids = jnp.arange(row_count, dtype=jnp.int32)
    starts = jnp.min(jnp.where(member, row_ids[None, :], row_count), axis=1)
    cosines, sines = rope_tables(CONTEXT + pair)

    group = group_index.reshape(1)
    packed = pack_pages(page_table[0], prior_len[0], cache_k, cache_v)
    pages = lax.all_to_all(packed, "req", split_axis=0, concat_axis=0, tiled=True)
    query, fresh = project(starts, counts, after(hidden_in, cosines, sines), attn_gain, w_query, w_key, w_value, pair)
    if peers == 8:
        side_down = swap(rows_of(w_down, group_index, groups), "req", peers, 1)
    mixed = attend(
        starts, counts, group, query, fresh, pages, cosines, sines, row_count, groups
    )
    new = lax.all_to_all(after(fresh, pages), "req", split_axis=0, concat_axis=0, tiled=True)
    if peers == 8:
        mixed, side_down, new = sync(mixed, side_down, new)

    out_of = lambda part: dot(part, w_out).astype(BF)
    to_home = functools.partial(swap, axis="grp", size=groups)
    cross = out_of(mixed[3])
    later = after(mixed, cross)
    cross = to_home(cross, bit=1)
    over = (out_of(later[2]).astype(F32) + cross.astype(F32)).astype(BF)
    over = to_home(over, bit=2)
    beside = to_home(out_of(later[1]), bit=1)
    own_rows = lax.dynamic_slice_in_dim(hidden_in, group_index * quarter, quarter, 0).astype(F32)
    near_sum = out_of(later[0]).astype(F32) + beside.astype(F32)
    residual, own, own_a, own_b = finish(own_rows + RESIDUAL_MULT * near_sum, over, mlp_gain)
    if peers == 8:
        held = [w_gate, w_up, w_down]
        down = exchange_mlp(own, own_a, own_b, peers, groups, group, held, side_down)
    else:
        piece = lax.all_gather(own, "req", axis=0, tiled=True)
        part = feed_forward(piece, w_gate, w_up, w_down)
        down = lax.psum_scatter(part, "req", scatter_dimension=0, tiled=True).astype(F32)
    keys_out, values_out = store_new(page_table[0], prior_len[0], new_len[0], new, cosines, sines, cache_k, cache_v)
    layer_out = (residual + RESIDUAL_MULT * down).astype(BF)
    return (layer_out, keys_out, values_out)


def solution(mesh):
    in_specs = (
        P("req", None),
        P(),
        P(),
        P(None, "grp"),
        P(None, "grp"),
        P(None, "grp"),
        P("grp", None),
        P(None, "req"),
        P(None, "req"),
        P("req", None),
        P("req", None, "grp"),
        P("req", None, "grp"),
        P("req"),
        P("req", None),
        P("req", None),
        P("req", None),
    )
    out_specs = (P(("req", "grp"), None), P("req", None, "grp"), P("req", None, "grp"))
    return jax.shard_map(body, mesh=mesh, in_specs=in_specs, out_specs=out_specs, check_vma=False)
```
